32 devices in a mesh: fsdp: 4 (over y, x), tp: 8 (over z, core).
Axes of the slice: x: 2, y: 2, z: 4, core: 2. Of those that a mesh axis runs over, the one named last changes fastest.
Arguments:
- prefix_states: bfloat16 [16384, 8192], P('fsdp', 'tp'), may hold values from -40 to 40
- new_states: bfloat16 [64, 8192], P('fsdp', 'tp'), may hold values from -40 to 40
- w_query: bfloat16 [8192, 8192], P('tp', 'fsdp'), may hold values from -0.09375 to 0.09375
- w_keyvalue: bfloat16 [8192, 2048], P('tp', 'fsdp'), may hold values from -0.03125 to 0.03125
- w_output: bfloat16 [8192, 8192], P('tp', 'fsdp'), may hold values from -0.25 to 0.25
- lengths: int32 [4, 4], P('fsdp'), may hold values from 1 to 1024, 3072 in all within a row
Outputs:
- kv_cache: bfloat16 [16384, 2048], P('fsdp', 'tp')
- mixed: bfloat16 [64, 8192], P('fsdp', 'tp')
The draws below stay inside these ranges and needn't reach their ends.
Inputs may be any that keep to these rules, and one draw needn't show every extreme that they name: `lengths`: in every group some sequence has length 1024.
All inputs are finite; a program needn't handle non-finite values.
Results may differ from the reference program's by a relative error of at most 0.02.
Values may be sent and summed in bfloat16 or wider, within the bound.
A program may use at most 128 MiB of HBM per device.

```python
import math
import jax
import jax.numpy as jnp
import numpy as np
from jax import lax

D = 8192
HQ = 64
KVH = 8
HD = 128
NSEQ = 4
L = 1024
STEPS = 4
GROUPS = 4
PREFIX_ROWS = 16384
FRESH_ROWS = 64
N_FSDP = 4
N_TP = 8


def draw_states(key, row_count, salt_value):
    noise_key = jax.random.fold_in(key, salt_value)
    values = jax.random.normal(jax.random.fold_in(noise_key, 4), (row_count, D), jnp.float32)
    return jnp.clip(values, -40.0, 40.0).astype(jnp.bfloat16)


def draw_prefix_states(key, part):
    return draw_states(key, PREFIX_ROWS, 101)


def draw_new_states(key, part):
    return draw_states(key, FRESH_ROWS, 202)


def with_spikes(drawn, own_key, source, target, blocks, factor):
    def block_of(dim):
        return (jnp.arange(drawn.shape[dim]) // (drawn.shape[dim] // blocks)).reshape((-1,) + (1,) * (drawn.ndim - 1 - dim))

    near = jax.random.permutation(own_key, blocks)[block_of(target)]
    far = (block_of(target) + blocks // 2) % blocks
    return jnp.where((block_of(source) == near) | (block_of(source) == far), factor * drawn, drawn)


def level_of(own_key, extent, cuts, low, high):
    gain = 1.0
    for position, parts in cuts:
        draws = jax.random.uniform(jax.random.fold_in(jax.random.fold_in(own_key, 6), position), (parts,), jnp.float32, low / len(cuts), high / len(cuts))
        gain = gain * jnp.repeat(jnp.exp(draws), extent[position] // parts).reshape((-1,) + (1,) * (len(extent) - 1 - position))
    return gain


def length_profile(number_of, total, bound, slope):
    weights = [(1 << 20) // math.isqrt(grade ** slope) + 1 for grade in range(2, number_of + 1)]
    spare, given = total - bound - (number_of - 1), [1] * (number_of - 1)
    while spare > 0:
        movable = [i for i in range(number_of - 1) if given[i] < bound]
        mass, remaining = sum([weights[i] for i in movable]), spare
        for i in movable:
            addition = min(bound - given[i], max(1, remaining * weights[i] // mass), spare)
            given[i] = given[i] + addition
            spare = spare - addition
    return np.array([bound] + given)


def ragged(key, number_of, total, most, lean):
    if number_of == 2:
        one = jax.random.randint(key, (), max(1, total - most), min(most, total - 1) + 1)
        return jnp.stack([one, total - one])
    sizes = jnp.asarray(length_profile(number_of, total, most, lean), jnp.int32)
    pairs = (number_of - 1) // 2
    donor, taker = sizes[1:1 + 2 * pairs:2], sizes[2:2 + 2 * pairs:2]
    margin = jnp.minimum(donor - 1, most - taker)
    passed = jax.random.randint(jax.random.fold_in(key, 1), (pairs,), 0, 1 << 20) % (margin + 1)
    sizes = sizes.at[1:1 + 2 * pairs:2].set(donor - passed).at[2:2 + 2 * pairs:2].set(taker + passed)
    return sizes[jax.random.permutation(jax.random.fold_in(key, 2), number_of)]


def bell_draw_with(stream_key, extent, spread, reach, pieces, heavy, kind=jnp.bfloat16):
    values = spread * jax.random.normal(stream_key, extent, jnp.float32)
    if pieces:
        values = values * level_of(stream_key, extent, pieces, -0.22, 0.18)
    return jnp.clip(with_spikes(values, jax.random.fold_in(stream_key, 3), *heavy), -reach, reach).astype(kind)


def setup_inputs(seed: int = 0) -> dict:
    seeds = jax.random.split(jax.random.key(seed), 7)
    prefix_states = draw_prefix_states(jax.random.fold_in(seeds[6], 71), 0)
    new_states = draw_new_states(jax.random.fold_in(seeds[6], 71), 0)
    w_query = bell_draw_with(seeds[2], (D, HQ * HD), D ** -0.5, 0.09375, ((0, 8), (1, 4)), (0, 1, 8, 2.0))
    w_keyvalue = bell_draw_with(seeds[3], (D, 2 * KVH * HD), (8 * D) ** -0.5, 0.03125, ((0, 8), (1, 4)), (0, 1, 8, 2.0))
    w_output = bell_draw_with(seeds[4], (HQ * HD, D), (HQ * HD // 8) ** -0.5, 0.25, ((0, 8), (1, 4)), (0, 1, 8, 2.0))
    lengths = jax.vmap(lambda own: ragged(own, NSEQ, 3 * NSEQ * L // 4, L, 1))(jax.random.split(seeds[5], GROUPS)).reshape((GROUPS, NSEQ)).astype(jnp.int32)
    return dict(prefix_states=prefix_states, new_states=new_states, w_query=w_query, w_keyvalue=w_keyvalue, w_output=w_output, lengths=lengths)


theta_base = 500000.0


def rotate(values, positions):
    half_dim = values.shape[-1] // 2
    frequency = theta_base ** (-2.0 * jnp.arange(half_dim, dtype=jnp.float32) / values.shape[-1])
    angles = positions[:, None, None] * frequency[None, None, :]
    cosine = jnp.cos(angles)
    sine_part = jnp.sin(angles)
    lower_half = values[..., :half_dim]
    upper_half = values[..., half_dim:]
    return jnp.concatenate([lower_half * cosine - upper_half * sine_part, upper_half * cosine + lower_half * sine_part], axis=-1)


def one_group(prefix_rows, fresh_rows, seq_lengths, w_query, w_keyvalue, w_output):
    token_count = prefix_rows.shape[0]
    fresh_count = fresh_rows.shape[0]
    block_width = D // N_TP
    kv_total = jnp.zeros((token_count, 2 * KVH * HD), jnp.float32)
    for block_index in range(N_TP):
        low_edge = block_index * block_width
        partial_kv = jnp.dot(prefix_rows[:, low_edge:low_edge + block_width], w_keyvalue[low_edge:low_edge + block_width], preferred_element_type=jnp.float32)
        kv_total = kv_total + lax.optimization_barrier(partial_kv.astype(jnp.bfloat16)).astype(jnp.float32)
    kv_heads = kv_total.reshape(token_count, KVH, 2, HD)
    slot_positions = (jnp.arange(token_count, dtype=jnp.int32) % L).astype(jnp.float32)
    rotated_keys = rotate(kv_heads[:, :, 0, :], slot_positions)
    cache = jnp.stack([rotated_keys, kv_heads[:, :, 1, :]], axis=2).reshape(token_count, 2 * KVH * HD).astype(jnp.bfloat16)
    query_sum = jnp.dot(fresh_rows, w_query, preferred_element_type=jnp.float32)
    new_kv = jnp.dot(fresh_rows, w_keyvalue, preferred_element_type=jnp.float32).reshape(fresh_count, KVH, 2, HD)
    fresh_positions = (jnp.repeat(seq_lengths, STEPS) + jnp.tile(jnp.arange(STEPS, dtype=jnp.int32), NSEQ)).astype(jnp.float32)
    query = rotate(query_sum.reshape(fresh_count, HQ, HD), fresh_positions).astype(jnp.bfloat16)
    new_keys = rotate(new_kv[:, :, 0, :], fresh_positions).astype(jnp.bfloat16)
    new_values = new_kv[:, :, 1, :].astype(jnp.bfloat16)
    cache_heads = cache.reshape(NSEQ, L, KVH, 2, HD).astype(jnp.float32)
    prefix_keys = cache_heads[:, :, :, 0, :]
    prefix_values = cache_heads[:, :, :, 1, :]
    query_five = query.astype(jnp.float32).reshape(NSEQ, STEPS, KVH, HQ // KVH, HD)
    score_scale = HD ** -0.5
    prefix_scores = jnp.einsum('sjkgd,slkd->sjkgl', query_five, prefix_keys, precision=lax.Precision.HIGHEST) * score_scale
    live_keys = jnp.arange(L, dtype=jnp.int32)[None, :] < seq_lengths[:, None]
    prefix_scores = jnp.where(live_keys[:, None, None, None, :], prefix_scores, -jnp.inf)
    fresh_keys = new_keys.astype(jnp.float32).reshape(NSEQ, STEPS, KVH, HD)
    fresh_values = new_values.astype(jnp.float32).reshape(NSEQ, STEPS, KVH, HD)
    fresh_scores = jnp.einsum('sjkgd,sikd->sjkgi', query_five, fresh_keys, precision=lax.Precision.HIGHEST) * score_scale
    causal = jnp.arange(STEPS)[None, :] <= jnp.arange(STEPS)[:, None]
    fresh_scores = jnp.where(causal[None, :, None, None, :], fresh_scores, -jnp.inf)
    row_max = jnp.maximum(jnp.max(prefix_scores, axis=-1), jnp.max(fresh_scores, axis=-1))
    prefix_weight = jnp.exp(prefix_scores - row_max[..., None])
    fresh_weight = jnp.exp(fresh_scores - row_max[..., None])
    denominator = jnp.sum(prefix_weight, axis=-1) + jnp.sum(fresh_weight, axis=-1)
    prefix_rounded = lax.optimization_barrier(prefix_weight.astype(jnp.bfloat16)).astype(jnp.float32)
    fresh_rounded = lax.optimization_barrier(fresh_weight.astype(jnp.bfloat16)).astype(jnp.float32)
    numerator = jnp.einsum('sjkgl,slkd->sjkgd', prefix_rounded, prefix_values, precision=lax.Precision.HIGHEST)
    numerator = numerator + jnp.einsum('sjkgi,sikd->sjkgd', fresh_rounded, fresh_values, precision=lax.Precision.HIGHEST)
    attended = (numerator / denominator[..., None]).reshape(fresh_count, HQ * HD).astype(jnp.bfloat16)
    mixed = jnp.dot(attended, w_output, preferred_element_type=jnp.float32).astype(jnp.bfloat16)
    return cache, mixed


def reference(prefix_states, new_states, w_query, w_keyvalue, w_output, lengths):
    prefix_groups = prefix_states.reshape(N_FSDP, NSEQ * L, D)
    fresh_groups = new_states.reshape(N_FSDP, NSEQ * STEPS, D)

    def run_group(packed):
        return one_group(packed[0], packed[1], packed[2], w_query, w_keyvalue, w_output)

    caches, outputs = lax.map(run_group, (prefix_groups, fresh_groups, lengths))
    return caches.reshape(N_FSDP * NSEQ * L, 2 * KVH * HD), outputs.reshape(N_FSDP * NSEQ * STEPS, D)
```

```python
import jax
import jax.numpy as jnp
from jax import lax
from jax.sharding import PartitionSpec as P

HD = 128
NSEQ = 4
L = 1024
STEPS = 4


theta_base = 500000.0
masked_score = -1e30


def partner(block, axis, apart):
    count = lax.axis_size(axis)
    route = []
    for low in range(count):
        high = low | 1 << apart
        if high != low and high < count:
            route += [(low, high), (high, low)]
    return lax.ppermute(block, axis, route)


def rotate(values, positions):
    half_dim = values.shape[-1] // 2
    frequency = theta_base ** (-2.0 * jnp.arange(half_dim, dtype=jnp.float32) / values.shape[-1])
    angles = positions[:, None, None] * frequency[None, None, :]
    cosine = jnp.cos(angles)
    sine_part = jnp.sin(angles)
    lower_half = values[..., :half_dim]
    upper_half = values[..., half_dim:]
    return jnp.concatenate(
        [
            lower_half * cosine - upper_half * sine_part,
            upper_half * cosine + lower_half * sine_part,
        ],
        axis=-1,
    )


def rotate_columns(column_table, positions):
    half_dim = column_table.shape[0] // 2
    frequency = theta_base ** (
        -2.0 * jnp.arange(half_dim, dtype=jnp.float32) / column_table.shape[0]
    )
    angles = frequency[:, None] * positions[None, :]
    cosine = jnp.cos(angles)
    sine_part = jnp.sin(angles)
    lower_half = column_table[:half_dim]
    upper_half = column_table[half_dim:]
    return jnp.concatenate(
        [
            lower_half * cosine - upper_half * sine_part,
            upper_half * cosine + lower_half * sine_part,
        ],
        axis=0,
    )


def by_owner(term):
    groups = lax.axis_size("fsdp")
    share = lax.axis_size("tp") // groups
    rows, columns = term.shape[0] // groups, term.shape[1] // share
    blocks = term.reshape(groups, rows, share, columns).transpose(0, 2, 1, 3)
    return blocks.reshape(groups * share, rows, columns)


def to_owners(blocks):
    groups, members = lax.axis_size("fsdp"), lax.axis_size("tp")
    share = members // groups
    mine = lax.psum_scatter(blocks, "tp", scatter_dimension=0, tiled=False)
    route = []
    for f in range(groups):
        for t in range(members):
            route.append((f * members + t, (t // share) * members + f * share + t % share))
    return lax.ppermute(mine, ("fsdp", "tp"), route)


def body(prefix_states, new_states, w_query, w_keyvalue, w_output, lengths):
    tp_count = lax.axis_size("tp")
    my_index = lax.axis_index("tp")
    token_count = prefix_states.shape[0]
    fresh_count = new_states.shape[0]
    seq_lengths = lengths[0]
    score_scale = HD ** (-0.5)
    kv_weight = lax.all_gather(w_keyvalue, "fsdp", axis=1, tiled=True)
    kv_width = kv_weight.shape[1]
    all_fresh = lax.all_gather(new_states, "fsdp", axis=0, tiled=True)
    query_term = jnp.dot(all_fresh, w_query, preferred_element_type=jnp.float32)
    fresh_term = jnp.dot(all_fresh, w_keyvalue, preferred_element_type=jnp.float32)
    fresh_positions = (
        jnp.repeat(seq_lengths, STEPS) + jnp.tile(jnp.arange(STEPS, dtype=jnp.int32), NSEQ)
    ).astype(jnp.float32)
    own_rows = kv_width // tp_count
    block_count = own_rows // HD
    block_kind = (my_index * block_count + jnp.arange(block_count, dtype=jnp.int32)) % 2
    cache_sum = lax.psum_scatter(
        lax.dot_general(
            kv_weight, prefix_states, (((0,), (1,)), ((), ())), preferred_element_type=jnp.float32
        ).astype(jnp.bfloat16),
        "tp",
        scatter_dimension=0,
        tiled=True,
    ).astype(jnp.float32)
    slot_positions = (jnp.arange(token_count, dtype=jnp.int32) % L).astype(jnp.float32)
    cache_blocks = cache_sum.reshape(block_count, HD, token_count)
    rotated_blocks = jax.vmap(lambda block_data: rotate_columns(block_data, slot_positions))(
        cache_blocks
    )
    cache_mine = jnp.where((block_kind == 0)[:, None, None], rotated_blocks, cache_blocks).astype(
        jnp.bfloat16
    )
    new_sum = to_owners(
        jnp.concatenate([by_owner(query_term), by_owner(fresh_term)], axis=2)
    )
    query_width = new_sum.shape[1] - own_rows
    query_sum, fresh_sum = new_sum[:, :query_width], new_sum[:, query_width:]
    fresh_blocks = fresh_sum.reshape(fresh_count, block_count, HD)
    fresh_rotated = rotate(fresh_blocks, fresh_positions)
    fresh_mine = jnp.where((block_kind == 0)[None, :, None], fresh_rotated, fresh_blocks).astype(
        jnp.bfloat16
    )
    if block_count == 1:
        cache_other, fresh_other = partner((cache_mine, fresh_mine), "tp", 0)
        holds_keys = my_index % 2 == 0
        key_table = jnp.where(holds_keys, cache_mine[0], cache_other[0])
        value_table = jnp.where(holds_keys, cache_other[0], cache_mine[0])
        fresh_keys = jnp.where(holds_keys, fresh_mine[:, 0], fresh_other[:, 0])
        fresh_values = jnp.where(holds_keys, fresh_other[:, 0], fresh_mine[:, 0])
    else:
        key_table = cache_mine[0]
        value_table = cache_mine[1]
        fresh_keys = fresh_mine[:, 0]
        fresh_values = fresh_mine[:, 1]
    cache_out = cache_mine.reshape(own_rows, token_count).T
    local_heads = query_sum.shape[1] // HD
    query_rot = rotate(query_sum.reshape(fresh_count, local_heads, HD), fresh_positions).astype(
        jnp.bfloat16
    )
    query_four = query_rot.reshape(NSEQ, STEPS, local_heads, HD)
    prefix_scores = (
        jnp.einsum(
            "sjhd,dsl->sjhl",
            query_four,
            key_table.reshape(HD, NSEQ, L),
            preferred_element_type=jnp.float32,
        )
        * score_scale
    )
    live_keys = jnp.arange(L, dtype=jnp.int32)[None, :] < seq_lengths[:, None]
    prefix_scores = jnp.where(live_keys[:, None, None, :], prefix_scores, masked_score)
    fresh_scores = (
        jnp.einsum(
            "sjhd,sid->sjhi",
            query_four,
            fresh_keys.reshape(NSEQ, STEPS, HD),
            preferred_element_type=jnp.float32,
        )
        * score_scale
    )
    causal = jnp.arange(STEPS)[None, :] <= jnp.arange(STEPS)[:, None]
    fresh_scores = jnp.where(causal[None, :, None, :], fresh_scores, masked_score)
    row_max = jnp.maximum(jnp.max(prefix_scores, axis=-1), jnp.max(fresh_scores, axis=-1))
    prefix_weight = jnp.exp(prefix_scores - row_max[..., None])
    fresh_weight = jnp.exp(fresh_scores - row_max[..., None])
    denominator = jnp.sum(prefix_weight, axis=-1) + jnp.sum(fresh_weight, axis=-1)
    numerator = jnp.einsum(
        "sjhl,dsl->sjhd",
        prefix_weight.astype(jnp.bfloat16),
        value_table.reshape(HD, NSEQ, L),
        preferred_element_type=jnp.float32,
    )
    numerator = numerator + jnp.einsum(
        "sjhi,sid->sjhd",
        fresh_weight.astype(jnp.bfloat16),
        fresh_values.reshape(NSEQ, STEPS, HD),
        preferred_element_type=jnp.float32,
    )
    attended = (
        (numerator / denominator[..., None])
        .reshape(fresh_count, local_heads * HD)
        .astype(jnp.bfloat16)
    )
    output_term = jnp.dot(
        lax.all_gather(attended, "fsdp", axis=0, tiled=True),
        w_output,
        preferred_element_type=jnp.float32,
    )
    mixed = to_owners(by_owner(output_term))
    return (cache_out, mixed.astype(jnp.bfloat16))


def solution(mesh):
    in_specs = (
        P("fsdp", "tp"),
        P("fsdp", "tp"),
        P("tp", "fsdp"),
        P("tp", "fsdp"),
        P("tp", "fsdp"),
        P("fsdp", None),
    )
    out_specs = (P("fsdp", "tp"), P("fsdp", "tp"))
    return jax.shard_map(body, mesh=mesh, in_specs=in_specs, out_specs=out_specs, check_vma=False)
```

```python
import functools

import jax
import jax.numpy as jnp
from jax import lax
from jax.experimental import pallas as pl
from jax.experimental.pallas import tpu as pltpu
from jax.sharding import PartitionSpec as P

HD = 128
NSEQ = 4
L = 1024
STEPS = 4
MESH = pl.DeviceIdType.MESH
VMEM = pl.BlockSpec(memory_space=pltpu.VMEM)


theta_base = 500000.0
masked_score = -1e30


def partner(block, axis, apart):
    count = lax.axis_size(axis)
    route = []
    for low in range(count):
        high = low | 1 << apart
        if high != low and high < count:
            route += [(low, high), (high, low)]
    return lax.ppermute(block, axis, route)


def rotate(values, positions):
    half_dim = values.shape[-1] // 2
    frequency = theta_base ** (-2.0 * jnp.arange(half_dim, dtype=jnp.float32) / values.shape[-1])
    angles = positions[:, None, None] * frequency[None, None, :]
    cosine = jnp.cos(angles)
    sine_part = jnp.sin(angles)
    lower_half = values[..., :half_dim]
    upper_half = values[..., half_dim:]
    return jnp.concatenate(
        [
            lower_half * cosine - upper_half * sine_part,
            upper_half * cosine + lower_half * sine_part,
        ],
        axis=-1,
    )


def flip(number, other, bits):
    result = 0
    for b in range(bits):
        one = lax.rem(lax.div(number, 1 << b), 2)
        two = lax.rem(lax.div(other, 1 << b), 2) if not isinstance(other, int) else (other >> b) & 1
        result = result + (one + two - 2 * one * two) * (1 << b)
    return result


def cache_kernel(groups, chips, pieces, x_ref, w_ref, cos_ref, sin_ref, out_ref,
                 x_other, w_all, arrived, leaving, total,
                 x_send, x_recv, w_send, w_recv, sum_send, sum_recv):
    bits = (groups - 1).bit_length()
    f = lax.axis_index("fsdp")
    t = lax.axis_index("tp")
    c = lax.div(t, 2)
    e = lax.rem(t, 2)
    token_count = x_ref.shape[0]
    rows = token_count // pieces
    own = out_ref.shape[1]
    table_rows = cos_ref.shape[0]

    def piece(k):
        return pl.ds(pl.multiple_of(k * rows, rows), rows)

    def half(which):
        return pl.ds(pl.multiple_of(which * own, own), own)

    def x_copy(k):
        return pltpu.make_async_remote_copy(
            src_ref=x_ref.at[piece(k)], dst_ref=x_other.at[piece(k)],
            send_sem=x_send.at[k], recv_sem=x_recv.at[k],
            device_id=(f, 2 * c + 1 - e), device_id_type=MESH)

    def w_copy(j, swap):
        core = e if swap == 0 else 1 - e
        return pltpu.make_async_remote_copy(
            src_ref=w_ref.at[:, half(core)], dst_ref=w_all.at[j, swap],
            send_sem=w_send.at[j, swap], recv_sem=w_recv.at[j, swap],
            device_id=(flip(f, j, bits), 2 * c + core), device_id_type=MESH)

    def sum_copy(j, k, slot, chip):
        return pltpu.make_async_remote_copy(
            src_ref=leaving.at[j, piece(k)], dst_ref=arrived.at[slot, piece(k)],
            send_sem=sum_send.at[j, k], recv_sem=sum_recv.at[slot, k],
            device_id=(f, 2 * chip + e), device_id_type=MESH)

    barrier = pltpu.get_barrier_semaphore()
    for j in range(groups):
        for swap in range(2):
            if j or swap:
                core = e if swap == 0 else 1 - e
                pl.semaphore_signal(barrier, inc=1, device_id=(flip(f, j, bits), 2 * c + core),
                                    device_id_type=MESH)

    @pl.when(c > 0)
    def _():
        pl.semaphore_signal(barrier, inc=1, device_id=(f, t - 2), device_id_type=MESH)

    @pl.when(c < chips - 1)
    def _():
        pl.semaphore_signal(barrier, inc=1, device_id=(f, t + 2), device_id_type=MESH)

    pl.semaphore_wait(barrier, 2 * groups - 1 + jnp.minimum(c, 1) + jnp.minimum(chips - 1 - c, 1))

    w_copy(0, 1).start()
    for j in range(1, groups):
        for swap in range(2):
            w_copy(j, swap).start()

    @pl.loop(0, pieces)
    def _(k):
        x_copy(k).start()

    w_all[0, 0] = w_ref[:, half(e)]
    w_copy(0, 1).wait_recv()

    @pl.loop(0, groups)
    def _(j):
        d = flip(f, j, bits)

        @pl.when(j > 0)
        def _():
            for swap in range(2):
                pltpu.make_async_remote_copy(
                    src_ref=w_ref.at[:, half(0)], dst_ref=w_all.at[j, swap],
                    send_sem=w_send.at[j, swap], recv_sem=w_recv.at[j, swap],
                    device_id=(f, 2 * c + 1 - e), device_id_type=MESH).wait_recv()

        @pl.loop(0, pieces)
        def _(k):
            @pl.when(j == 0)
            def _():
                x_copy(k).wait_recv()

            term = jnp.dot(x_ref[piece(k)], w_all[j, 0], preferred_element_type=jnp.float32)
            term += jnp.dot(x_other[piece(k)], w_all[j, 1], preferred_element_type=jnp.float32)

            @pl.when(d == c)
            def _():
                total[piece(k)] = term

            @pl.when(d > c)
            def _():
                @pl.when(c > 0)
                def _():
                    sum_copy(j, k, j, c + 1).wait_recv()
                    leaving[j, piece(k)] = (term + arrived[j, piece(k)].astype(jnp.float32)).astype(jnp.bfloat16)

                @pl.when(c == 0)
                def _():
                    leaving[j, piece(k)] = term.astype(jnp.bfloat16)

                sum_copy(j, k, j, c + 1).start()

            @pl.when(d < c)
            def _():
                @pl.when(c < chips - 1)
                def _():
                    sum_copy(j, k, j, c - 1).wait_recv()
                    leaving[j, piece(k)] = (term + arrived[j, piece(k)].astype(jnp.float32)).astype(jnp.bfloat16)

                @pl.when(c == chips - 1)
                def _():
                    leaving[j, piece(k)] = term.astype(jnp.bfloat16)

                @pl.when(d == c - 1)
                def _():
                    sum_copy(j, k, groups, c - 1).start()

                @pl.when(d < c - 1)
                def _():
                    sum_copy(j, k, j, c - 1).start()

    mine = flip(f, c, bits)

    @pl.loop(0, pieces)
    def _(k):
        @pl.when(c > 0)
        def _():
            sum_copy(mine, k, mine, c).wait_recv()
            total[piece(k)] += arrived[mine, piece(k)].astype(jnp.float32)

        @pl.when(c < chips - 1)
        def _():
            sum_copy(mine, k, groups, c).wait_recv()
            total[piece(k)] += arrived[groups, piece(k)].astype(jnp.float32)

        place = pl.ds(pl.multiple_of(lax.rem(k * rows, table_rows), rows), rows)
        for b in range(own // HD):
            cut = slice(b * HD, (b + 1) * HD)
            value = total[piece(k), cut]
            turned = value * cos_ref[place, cut] + pltpu.roll(value, HD // 2, 1) * sin_ref[place, cut]
            out_ref[piece(k), cut] = turned.astype(out_ref.dtype)

    w_copy(0, 1).wait_send()
    for j in range(1, groups):
        for swap in range(2):
            w_copy(j, swap).wait_send()

    @pl.loop(0, pieces)
    def _(k):
        x_copy(k).wait_send()

        @pl.loop(0, groups)
        def _(j):
            @pl.when(flip(f, j, bits) != c)
            def _():
                sum_copy(j, k, j, c).wait_send()


def recompute_cache(prefix_states, w_keyvalue, cosine, sine_part):
    groups, members = lax.axis_size("fsdp"), lax.axis_size("tp")
    chips = members // 2
    assert chips == groups and groups & (groups - 1) == 0
    token_count, depth = prefix_states.shape
    own = w_keyvalue.shape[1] // 2
    pieces = token_count // 256
    return pl.pallas_call(
        functools.partial(cache_kernel, groups, chips, pieces),
        out_shape=jax.ShapeDtypeStruct((token_count, own), jnp.bfloat16),
        in_specs=[VMEM] * 4,
        out_specs=VMEM,
        scratch_shapes=[
            pltpu.VMEM((token_count, depth), jnp.bfloat16),
            pltpu.VMEM((groups, 2, depth, own), jnp.bfloat16),
            pltpu.VMEM((groups + 1, token_count, own), jnp.bfloat16),
            pltpu.VMEM((groups, token_count, own), jnp.bfloat16),
            pltpu.VMEM((token_count, own), jnp.float32),
            pltpu.SemaphoreType.DMA((pieces,)),
            pltpu.SemaphoreType.DMA((pieces,)),
            pltpu.SemaphoreType.DMA((groups, 2)),
            pltpu.SemaphoreType.DMA((groups, 2)),
            pltpu.SemaphoreType.DMA((groups, pieces)),
            pltpu.SemaphoreType.DMA((groups + 1, pieces)),
        ],
        compiler_params=pltpu.CompilerParams(
            collective_id=0, has_side_effects=True, vmem_limit_bytes=56 * 1024 * 1024),
    )(prefix_states, w_keyvalue, cosine, sine_part)


def project_kernel(groups, members, x_ref, w_ref, out_ref, x_all, leaving, arrived,
                   x_send, x_recv, part_send, part_recv):
    share = members // groups
    f = lax.axis_index("fsdp")
    t = lax.axis_index("tp")
    home = lax.div(t, share)
    rows = x_ref.shape[0]
    columns = out_ref.shape[1]

    def x_copy(j):
        return pltpu.make_async_remote_copy(
            src_ref=x_ref, dst_ref=x_all.at[f],
            send_sem=x_send.at[j], recv_sem=x_recv.at[f],
            device_id=(lax.rem(f + j, groups), t), device_id_type=MESH)

    def part_copy(g, h):
        return pltpu.make_async_remote_copy(
            src_ref=leaving.at[h, pl.ds(pl.multiple_of(g * rows, rows), rows)],
            dst_ref=arrived.at[t],
            send_sem=part_send.at[g, h], recv_sem=part_recv.at[t],
            device_id=(g, f * share + h), device_id_type=MESH)

    barrier = pltpu.get_barrier_semaphore()
    for j in range(1, groups):
        pl.semaphore_signal(barrier, inc=1, device_id=(lax.rem(f + j, groups), t), device_id_type=MESH)
    for source in range(members):
        @pl.when(jnp.logical_or(home != f, source != t))
        def _():
            pl.semaphore_signal(barrier, inc=1, device_id=(home, source), device_id_type=MESH)

    pl.semaphore_wait(barrier, groups + members - 2 + jnp.minimum(jnp.abs(home - f), 1))

    for j in range(1, groups):
        x_copy(j).start()
    x_all[f] = x_ref[...]
    for j in range(1, groups):
        source = lax.rem(f + j, groups)
        pltpu.make_async_remote_copy(
            src_ref=x_ref, dst_ref=x_all.at[source],
            send_sem=x_send.at[j], recv_sem=x_recv.at[source],
            device_id=(source, t), device_id_type=MESH).wait_recv()
    x = x_all[...].reshape(groups * rows, x_ref.shape[1])
    for h in range(share):
        leaving[h] = jnp.dot(x, w_ref[:, h * columns:(h + 1) * columns],
                             preferred_element_type=jnp.float32)
        for g in range(groups):
            away = jnp.logical_or(f != g, t != f * share + h)

            @pl.when(away)
            def _():
                part_copy(g, h).start()

            @pl.when(jnp.logical_not(away))
            def _():
                arrived[t] = leaving[h, g * rows:(g + 1) * rows]

    result = jnp.zeros(out_ref.shape, jnp.float32)
    for source in range(members):
        @pl.when(jnp.logical_or(home != f, source != t))
        def _():
            pltpu.make_async_remote_copy(
                src_ref=leaving.at[0, pl.ds(0, rows)], dst_ref=arrived.at[source],
                send_sem=part_send.at[0, 0], recv_sem=part_recv.at[source],
                device_id=(f, lax.rem(t + 1, members)), device_id_type=MESH).wait_recv()
        result += arrived[source]
    out_ref[...] = result.astype(out_ref.dtype)
    for j in range(1, groups):
        x_copy(j).wait_send()
    for g in range(groups):
        for h in range(share):
            @pl.when(jnp.logical_or(f != g, t != f * share + h))
            def _():
                part_copy(g, h).wait_send()


def project(x, weight, out_dtype, collective_id):
    groups, members = lax.axis_size("fsdp"), lax.axis_size("tp")
    share = members // groups
    rows, depth = x.shape
    columns = weight.shape[1] // share
    return pl.pallas_call(
        functools.partial(project_kernel, groups, members),
        out_shape=jax.ShapeDtypeStruct((rows, columns), out_dtype),
        in_specs=[VMEM] * 2,
        out_specs=VMEM,
        scratch_shapes=[
            pltpu.VMEM((groups, rows, depth), x.dtype),
            pltpu.VMEM((share, groups * rows, columns), jnp.float32),
            pltpu.VMEM((members, rows, columns), jnp.float32),
            pltpu.SemaphoreType.DMA((groups,)),
            pltpu.SemaphoreType.DMA((groups,)),
            pltpu.SemaphoreType.DMA((groups, share)),
            pltpu.SemaphoreType.DMA((members,)),
        ],
        compiler_params=pltpu.CompilerParams(
            collective_id=collective_id, has_side_effects=True, vmem_limit_bytes=32 * 1024 * 1024),
    )(x, weight)


def by_owner(term):
    groups = lax.axis_size("fsdp")
    share = lax.axis_size("tp") // groups
    rows, columns = term.shape[0] // groups, term.shape[1] // share
    blocks = term.reshape(groups, rows, share, columns).transpose(0, 2, 1, 3)
    return blocks.reshape(groups * share, rows, columns)


def to_owners(blocks):
    groups, members = lax.axis_size("fsdp"), lax.axis_size("tp")
    share = members // groups
    mine = lax.psum_scatter(blocks, "tp", scatter_dimension=0, tiled=False)
    route = []
    for f in range(groups):
        for t in range(members):
            route.append((f * members + t, (t // share) * members + f * share + t % share))
    return lax.ppermute(mine, ("fsdp", "tp"), route)


def fresh_sums(new_states, w_query, w_keyvalue):
    all_fresh = lax.all_gather(new_states, "fsdp", axis=0, tiled=True)
    query_term = jnp.dot(all_fresh, w_query, preferred_element_type=jnp.float32)
    fresh_term = jnp.dot(all_fresh, w_keyvalue, preferred_element_type=jnp.float32)
    return to_owners(jnp.concatenate([by_owner(query_term), by_owner(fresh_term)], axis=2))


def body(prefix_states, new_states, w_query, w_keyvalue, w_output, lengths):
    my_index = lax.axis_index("tp")
    token_count = prefix_states.shape[0]
    fresh_count = new_states.shape[0]
    seq_lengths = lengths[0]
    score_scale = HD ** (-0.5)
    own_rows = w_keyvalue.shape[1] // 2
    block_count = own_rows // HD
    block_kind = (my_index * block_count + jnp.arange(block_count, dtype=jnp.int32)) % 2
    frequency = theta_base ** (-2.0 * jnp.arange(HD // 2, dtype=jnp.float32) / HD)
    angles = jnp.arange(L, dtype=jnp.int32).astype(jnp.float32)[:, None] * frequency[None, :]
    cosine, sine_part = jnp.cos(angles), jnp.sin(angles)
    is_key = jnp.repeat(block_kind == 0, HD)[None, :]
    cosine = jnp.where(is_key, jnp.tile(cosine, (1, 2 * block_count)), 1.0)
    sine_part = jnp.where(
        is_key, jnp.tile(jnp.concatenate([-sine_part, sine_part], axis=1), (1, block_count)), 0.0
    )
    new_sum = fresh_sums(new_states, w_query, w_keyvalue)
    query_width = new_sum.shape[1] - own_rows
    query_sum, fresh_sum = new_sum[:, :query_width], new_sum[:, query_width:]
    cache_out = recompute_cache(prefix_states, w_keyvalue, cosine, sine_part)
    fresh_positions = (
        jnp.repeat(seq_lengths, STEPS) + jnp.tile(jnp.arange(STEPS, dtype=jnp.int32), NSEQ)
    ).astype(jnp.float32)
    fresh_blocks = fresh_sum.reshape(fresh_count, block_count, HD)
    fresh_rotated = rotate(fresh_blocks, fresh_positions)
    fresh_mine = jnp.where((block_kind == 0)[None, :, None], fresh_rotated, fresh_blocks).astype(
        jnp.bfloat16
    )
    if block_count == 1:
        cache_other, fresh_other = partner((cache_out, fresh_mine), "tp", 0)
        holds_keys = my_index % 2 == 0
        key_table = jnp.where(holds_keys, cache_out, cache_other)
        value_table = jnp.where(holds_keys, cache_other, cache_out)
        fresh_keys = jnp.where(holds_keys, fresh_mine[:, 0], fresh_other[:, 0])
        fresh_values = jnp.where(holds_keys, fresh_other[:, 0], fresh_mine[:, 0])
    else:
        key_table = cache_out[:, :HD]
        value_table = cache_out[:, HD:]
        fresh_keys = fresh_mine[:, 0]
        fresh_values = fresh_mine[:, 1]
    local_heads = query_sum.shape[1] // HD
    query_rot = rotate(query_sum.reshape(fresh_count, local_heads, HD), fresh_positions).astype(
        jnp.bfloat16
    )
    query_four = query_rot.reshape(NSEQ, STEPS, local_heads, HD)
    prefix_scores = (
        jnp.einsum(
            "sjhd,sld->sjhl",
            query_four,
            key_table.reshape(NSEQ, L, HD),
            preferred_element_type=jnp.float32,
        )
        * score_scale
    )
    live_keys = jnp.arange(L, dtype=jnp.int32)[None, :] < seq_lengths[:, None]
    prefix_scores = jnp.where(live_keys[:, None, None, :], prefix_scores, masked_score)
    fresh_scores = (
        jnp.einsum(
            "sjhd,sid->sjhi",
            query_four,
            fresh_keys.reshape(NSEQ, STEPS, HD),
            preferred_element_type=jnp.float32,
        )
        * score_scale
    )
    causal = jnp.arange(STEPS)[None, :] <= jnp.arange(STEPS)[:, None]
    fresh_scores = jnp.where(causal[None, :, None, :], fresh_scores, masked_score)
    row_max = jnp.maximum(jnp.max(prefix_scores, axis=-1), jnp.max(fresh_scores, axis=-1))
    prefix_weight = jnp.exp(prefix_scores - row_max[..., None])
    fresh_weight = jnp.exp(fresh_scores - row_max[..., None])
    denominator = jnp.sum(prefix_weight, axis=-1) + jnp.sum(fresh_weight, axis=-1)
    numerator = jnp.einsum(
        "sjhl,sld->sjhd",
        prefix_weight.astype(jnp.bfloat16),
        value_table.reshape(NSEQ, L, HD),
        preferred_element_type=jnp.float32,
    )
    numerator = numerator + jnp.einsum(
        "sjhi,sid->sjhd",
        fresh_weight.astype(jnp.bfloat16),
        fresh_values.reshape(NSEQ, STEPS, HD),
        preferred_element_type=jnp.float32,
    )
    attended = (
        (numerator / denominator[..., None])
        .reshape(fresh_count, local_heads * HD)
        .astype(jnp.bfloat16)
    )
    return (cache_out, project(attended, w_output, jnp.bfloat16, 1))


def solution(mesh):
    in_specs = (
        P("fsdp", "tp"),
        P("fsdp", "tp"),
        P("tp", "fsdp"),
        P("tp", "fsdp"),
        P("tp", "fsdp"),
        P("fsdp", None),
    )
    out_specs = (P("fsdp", "tp"), P("fsdp", "tp"))
    return jax.shard_map(body, mesh=mesh, in_specs=in_specs, out_specs=out_specs, check_vma=False)
```

```python
import functools

import jax
import jax.numpy as jnp
from jax import lax
from jax.experimental import pallas as pl
from jax.experimental.pallas import tpu as pltpu
from jax.sharding import PartitionSpec as P

HD = 128
NSEQ = 4
L = 1024
STEPS = 4
MESH = pl.DeviceIdType.MESH
VMEM = pl.BlockSpec(memory_space=pltpu.VMEM)


theta_base = 500000.0
masked_score = -1e30


def partner(block, axis, apart):
    count = lax.axis_size(axis)
    route = []
    for low in range(count):
        high = low | 1 << apart
        if high != low and high < count:
            route += [(low, high), (high, low)]
    return lax.ppermute(block, axis, route)


def rotate(values, positions):
    half_dim = values.shape[-1] // 2
    frequency = theta_base ** (-2.0 * jnp.arange(half_dim, dtype=jnp.float32) / values.shape[-1])
    angles = positions[:, None, None] * frequency[None, None, :]
    cosine = jnp.cos(angles)
    sine_part = jnp.sin(angles)
    lower_half = values[..., :half_dim]
    upper_half = values[..., half_dim:]
    return jnp.concatenate(
        [
            lower_half * cosine - upper_half * sine_part,
            upper_half * cosine + lower_half * sine_part,
        ],
        axis=-1,
    )


def flip(number, other, bits):
    result = 0
    for b in range(bits):
        one = lax.rem(lax.div(number, 1 << b), 2)
        two = lax.rem(lax.div(other, 1 << b), 2) if not isinstance(other, int) else (other >> b) & 1
        result = result + (one + two - 2 * one * two) * (1 << b)
    return result


def relay(f, t, groups, members, x_ref, x_all, near_out, near_in, far_in, sems):
    x_send, x_recv, near_send, near_recv, far_send, far_recv = sems
    rows = x_ref.shape[0]
    share = members // groups

    def across(j):
        return lax.rem(f + j, groups)

    def along(i):
        return lax.rem(t + i, members)

    def x_copy(j, slot):
        return pltpu.make_async_remote_copy(
            src_ref=x_ref, dst_ref=x_all.at[slot], send_sem=x_send.at[j], recv_sem=x_recv.at[slot],
            device_id=(across(j), t), device_id_type=MESH)

    def near_copy(j, slot):
        return pltpu.make_async_remote_copy(
            src_ref=near_out.at[:, pl.ds(pl.multiple_of(across(j) * rows, rows), rows)],
            dst_ref=near_in.at[slot], send_sem=near_send.at[j], recv_sem=near_recv.at[slot],
            device_id=(across(j), t), device_id_type=MESH)

    def far_copy(i, slot):
        to = along(i)
        return pltpu.make_async_remote_copy(
            src_ref=near_in.at[lax.div(to, share), lax.rem(to, share)],
            dst_ref=far_in.at[slot], send_sem=far_send.at[i], recv_sem=far_recv.at[slot],
            device_id=(f, to), device_id_type=MESH)

    def gather():
        for j in range(1, groups):
            x_copy(j, f).start()
        x_all[f] = x_ref[...]

    def multiply(weights):
        for j in range(1, groups):
            x_copy(j, across(j)).wait_recv()
        x = x_all[...].reshape(groups * rows, x_ref.shape[1])
        for h in range(share):
            base = 0
            for w_ref in weights:
                width = w_ref.shape[1] // share
                near_out[h, :, base:base + width] = jnp.dot(
                    x, w_ref[:, h * width:(h + 1) * width], preferred_element_type=jnp.float32
                ).astype(near_out.dtype)
                base += width
        for j in range(1, groups):
            near_copy(j, f).start()
        near_in[f] = near_out[:, pl.ds(pl.multiple_of(f * rows, rows), rows)]

    def scatter():
        for j in range(1, groups):
            near_copy(j, across(j)).wait_recv()
        for i in range(1, members):
            far_copy(i, t).start()
        far_in[t] = near_in[lax.div(t, share), lax.rem(t, share)]

    def collect():
        for i in range(1, members):
            far_copy(i, along(i)).wait_recv()
        result = far_in[0].astype(jnp.float32)
        for source in range(1, members):
            result += far_in[source].astype(jnp.float32)
        return result

    def drain():
        for j in range(1, groups):
            x_copy(j, f).wait_send()
            near_copy(j, f).wait_send()
        for i in range(1, members):
            far_copy(i, t).wait_send()

    return gather, multiply, scatter, collect, drain


def relay_scratch(groups, members, rows, depth, columns):
    share = members // groups
    return [
        pltpu.VMEM((groups, rows, depth), jnp.bfloat16),
        pltpu.VMEM((share, groups * rows, columns), jnp.bfloat16),
        pltpu.VMEM((groups, share, rows, columns), jnp.bfloat16),
        pltpu.VMEM((members, rows, columns), jnp.bfloat16),
    ] + [pltpu.SemaphoreType.DMA((n,)) for n in (groups, groups, groups, groups, members, members)]


def cache_kernel(groups, chips, pieces, x_ref, w_ref, cos_ref, sin_ref, new_ref, wq_ref,
                 out_ref, new_out_ref,
                 x_other, w_all, arrived, leaving, total,
                 x_send, x_recv, w_send, w_recv, sum_send, sum_recv,
                 new_all, near_out, near_in, far_in, *relay_sems):
    members = 2 * chips
    bits = (groups - 1).bit_length()
    f = lax.axis_index("fsdp")
    t = lax.axis_index("tp")
    c = lax.div(t, 2)
    e = lax.rem(t, 2)
    token_count = x_ref.shape[0]
    rows = token_count // pieces
    own = out_ref.shape[1]
    table_rows = cos_ref.shape[0]
    gather, multiply, scatter, collect, drain = relay(
        f, t, groups, members, new_ref, new_all, near_out, near_in, far_in, relay_sems)

    def piece(k):
        return pl.ds(pl.multiple_of(k * rows, rows), rows)

    def half(which):
        return pl.ds(pl.multiple_of(which * own, own), own)

    def x_copy(k):
        return pltpu.make_async_remote_copy(
            src_ref=x_ref.at[piece(k)], dst_ref=x_other.at[piece(k)],
            send_sem=x_send.at[k], recv_sem=x_recv.at[k],
            device_id=(f, 2 * c + 1 - e), device_id_type=MESH)

    def w_copy(j, swap):
        core = e if swap == 0 else 1 - e
        return pltpu.make_async_remote_copy(
            src_ref=w_ref.at[:, half(core)], dst_ref=w_all.at[j, swap],
            send_sem=w_send.at[j, swap], recv_sem=w_recv.at[j, swap],
            device_id=(flip(f, j, bits), 2 * c + core), device_id_type=MESH)

    def sum_copy(j, k, slot, chip):
        return pltpu.make_async_remote_copy(
            src_ref=leaving.at[j, piece(k)], dst_ref=arrived.at[slot, piece(k)],
            send_sem=sum_send.at[j, k], recv_sem=sum_recv.at[slot, k],
            device_id=(f, 2 * chip + e), device_id_type=MESH)

    def send_right(j, k):
        sum_copy(j, k, j, c + 1).start()

    def send_left(j, k, d):
        @pl.when(d == c - 1)
        def _():
            sum_copy(j, k, groups, c - 1).start()

        @pl.when(d < c - 1)
        def _():
            sum_copy(j, k, j, c - 1).start()

    def add_arrived(j, k):
        sum_copy(j, k, j, c).wait_recv()
        leaving[j, piece(k)] = (
            leaving[j, piece(k)].astype(jnp.float32) + arrived[j, piece(k)].astype(jnp.float32)
        ).astype(jnp.bfloat16)

    barrier = pltpu.get_barrier_semaphore()
    for j in range(1, groups):
        for core in range(2):
            pl.semaphore_signal(barrier, inc=1, device_id=(flip(f, j, bits), 2 * c + core),
                                device_id_type=MESH)
    for i in range(1, members):
        pl.semaphore_signal(barrier, inc=1, device_id=(f, lax.rem(t + i, members)),
                            device_id_type=MESH)
    pl.semaphore_wait(barrier, 2 * (groups - 1) + members - 1)

    w_copy(0, 1).start()
    for j in range(1, groups):
        for swap in range(2):
            w_copy(j, swap).start()

    @pl.loop(0, pieces)
    def _(k):
        x_copy(k).start()

    gather()
    w_all[0, 0] = w_ref[:, half(e)]
    w_copy(0, 1).wait_recv()

    @pl.loop(0, groups)
    def _(j):
        d = flip(f, j, bits)

        @pl.when(j > 0)
        def _():
            for swap in range(2):
                pltpu.make_async_remote_copy(
                    src_ref=w_ref.at[:, half(0)], dst_ref=w_all.at[j, swap],
                    send_sem=w_send.at[j, swap], recv_sem=w_recv.at[j, swap],
                    device_id=(f, 2 * c + 1 - e), device_id_type=MESH).wait_recv()

        @pl.loop(0, pieces)
        def _(k):
            @pl.when(j == 0)
            def _():
                x_copy(k).wait_recv()

            term = jnp.dot(x_ref[piece(k)], w_all[j, 0], preferred_element_type=jnp.float32)
            term += jnp.dot(x_other[piece(k)], w_all[j, 1], preferred_element_type=jnp.float32)

            @pl.when(d == c)
            def _():
                total[piece(k)] = term

            @pl.when(d != c)
            def _():
                leaving[j, piece(k)] = term.astype(jnp.bfloat16)

                @pl.when(c == 0)
                def _():
                    send_right(j, k)

                @pl.when(c == chips - 1)
                def _():
                    send_left(j, k, d)

    multiply([wq_ref, w_ref])
    scatter()

    mine = flip(f, c, bits)
    from_right = flip(f, 0, bits)
    from_left = flip(f, chips - 1, bits)
    slot_right = mine - jnp.where(from_right < mine, 1, 0)
    slot_left = mine - jnp.where(from_left < mine, 1, 0)
    last = jnp.where(c == 0, slot_left, jnp.where(c == chips - 1, slot_right,
                                                  jnp.maximum(slot_left, slot_right)))

    def finish(k):
        @pl.when(c > 0)
        def _():
            sum_copy(mine, k, mine, c).wait_recv()
            total[piece(k)] += arrived[mine, piece(k)].astype(jnp.float32)

        @pl.when(c < chips - 1)
        def _():
            sum_copy(mine, k, groups, c).wait_recv()
            total[piece(k)] += arrived[groups, piece(k)].astype(jnp.float32)

        place = pl.ds(pl.multiple_of(lax.rem(k * rows, table_rows), rows), rows)
        for b in range(own // HD):
            cut = slice(b * HD, (b + 1) * HD)
            value = total[piece(k), cut]
            turned = value * cos_ref[place, cut] + pltpu.roll(value, HD // 2, 1) * sin_ref[place, cut]
            out_ref[piece(k), cut] = turned.astype(out_ref.dtype)

    @pl.loop(0, chips - 1)
    def _(slot):
        j_right = slot + jnp.where(from_right <= slot, 1, 0)
        j_left = slot + jnp.where(from_left <= slot, 1, 0)
        d_right = flip(f, j_right, bits)
        d_left = flip(f, j_left, bits)

        @pl.loop(0, pieces)
        def _(k):
            @pl.when(jnp.logical_and(c > 0, d_right > c))
            def _():
                add_arrived(j_right, k)
                send_right(j_right, k)

            @pl.when(jnp.logical_and(c < chips - 1, d_left < c))
            def _():
                add_arrived(j_left, k)
                send_left(j_left, k, d_left)

            @pl.when(slot == last)
            def _():
                finish(k)

    new_out_ref[...] = collect()
    drain()
    w_copy(0, 1).wait_send()
    for j in range(1, groups):
        for swap in range(2):
            w_copy(j, swap).wait_send()

    @pl.loop(0, pieces)
    def _(k):
        x_copy(k).wait_send()

        @pl.loop(0, groups)
        def _(j):
            @pl.when(flip(f, j, bits) != c)
            def _():
                sum_copy(j, k, j, c).wait_send()


def recompute_cache(prefix_states, w_keyvalue, cosine, sine_part, new_states, w_query):
    groups, members = lax.axis_size("fsdp"), lax.axis_size("tp")
    chips = members // 2
    assert chips == groups and groups & (groups - 1) == 0
    token_count, depth = prefix_states.shape
    own = w_keyvalue.shape[1] // 2
    pieces = token_count // 256
    fresh_count = new_states.shape[0]
    fresh_width = (w_query.shape[1] + w_keyvalue.shape[1]) * groups // members
    return pl.pallas_call(
        functools.partial(cache_kernel, groups, chips, pieces),
        out_shape=(
            jax.ShapeDtypeStruct((token_count, own), jnp.bfloat16),
            jax.ShapeDtypeStruct((fresh_count, fresh_width), jnp.float32),
        ),
        in_specs=[VMEM] * 6,
        out_specs=(VMEM, VMEM),
        scratch_shapes=[
            pltpu.VMEM((token_count, depth), jnp.bfloat16),
            pltpu.VMEM((groups, 2, depth, own), jnp.bfloat16),
            pltpu.VMEM((groups + 1, token_count, own), jnp.bfloat16),
            pltpu.VMEM((groups, token_count, own), jnp.bfloat16),
            pltpu.VMEM((token_count, own), jnp.float32),
            pltpu.SemaphoreType.DMA((pieces,)),
            pltpu.SemaphoreType.DMA((pieces,)),
            pltpu.SemaphoreType.DMA((groups, 2)),
            pltpu.SemaphoreType.DMA((groups, 2)),
            pltpu.SemaphoreType.DMA((groups, pieces)),
            pltpu.SemaphoreType.DMA((groups + 1, pieces)),
        ] + relay_scratch(groups, members, fresh_count, depth, fresh_width),
        compiler_params=pltpu.CompilerParams(
            collective_id=0, has_side_effects=True, vmem_limit_bytes=60 * 1024 * 1024),
    )(prefix_states, w_keyvalue, cosine, sine_part, new_states, w_query)


def project_kernel(groups, members, x_ref, w_ref, out_ref, x_all, near_out, near_in, far_in, *sems):
    f = lax.axis_index("fsdp")
    t = lax.axis_index("tp")
    barrier = pltpu.get_barrier_semaphore()
    for j in range(1, groups):
        pl.semaphore_signal(barrier, inc=1, device_id=(lax.rem(f + j, groups), t),
                            device_id_type=MESH)
    for i in range(1, members):
        pl.semaphore_signal(barrier, inc=1, device_id=(f, lax.rem(t + i, members)),
                            device_id_type=MESH)
    pl.semaphore_wait(barrier, groups + members - 2)
    gather, multiply, scatter, collect, drain = relay(
        f, t, groups, members, x_ref, x_all, near_out, near_in, far_in, sems)
    gather()
    multiply([w_ref])
    scatter()
    out_ref[...] = collect().astype(out_ref.dtype)
    drain()


def project(x, weight, out_dtype, collective_id):
    groups, members = lax.axis_size("fsdp"), lax.axis_size("tp")
    rows, depth = x.shape
    columns = weight.shape[1] * groups // members
    return pl.pallas_call(
        functools.partial(project_kernel, groups, members),
        out_shape=jax.ShapeDtypeStruct((rows, columns), out_dtype),
        in_specs=[VMEM] * 2,
        out_specs=VMEM,
        scratch_shapes=relay_scratch(groups, members, rows, depth, columns),
        compiler_params=pltpu.CompilerParams(
            collective_id=collective_id, has_side_effects=True, vmem_limit_bytes=32 * 1024 * 1024),
    )(x, weight)


def body(prefix_states, new_states, w_query, w_keyvalue, w_output, lengths):
    my_index = lax.axis_index("tp")
    token_count = prefix_states.shape[0]
    fresh_count = new_states.shape[0]
    seq_lengths = lengths[0]
    score_scale = HD ** (-0.5)
    own_rows = w_keyvalue.shape[1] // 2
    block_count = own_rows // HD
    block_kind = (my_index * block_count + jnp.arange(block_count, dtype=jnp.int32)) % 2
    frequency = theta_base ** (-2.0 * jnp.arange(HD // 2, dtype=jnp.float32) / HD)
    angles = jnp.arange(L, dtype=jnp.int32).astype(jnp.float32)[:, None] * frequency[None, :]
    cosine, sine_part = jnp.cos(angles), jnp.sin(angles)
    is_key = jnp.repeat(block_kind == 0, HD)[None, :]
    cosine = jnp.where(is_key, jnp.tile(cosine, (1, 2 * block_count)), 1.0)
    sine_part = jnp.where(
        is_key, jnp.tile(jnp.concatenate([-sine_part, sine_part], axis=1), (1, block_count)), 0.0
    )
    cache_out, new_sum = recompute_cache(
        prefix_states, w_keyvalue, cosine, sine_part, new_states, w_query
    )
    query_width = new_sum.shape[1] - own_rows
    query_sum, fresh_sum = new_sum[:, :query_width], new_sum[:, query_width:]
    fresh_positions = (
        jnp.repeat(seq_lengths, STEPS) + jnp.tile(jnp.arange(STEPS, dtype=jnp.int32), NSEQ)
    ).astype(jnp.float32)
    fresh_blocks = fresh_sum.reshape(fresh_count, block_count, HD)
    fresh_rotated = rotate(fresh_blocks, fresh_positions)
    fresh_mine = jnp.where((block_kind == 0)[None, :, None], fresh_rotated, fresh_blocks).astype(
        jnp.bfloat16
    )
    if block_count == 1:
        cache_other, fresh_other = partner((cache_out, fresh_mine), "tp", 0)
        holds_keys = my_index % 2 == 0
        key_table = jnp.where(holds_keys, cache_out, cache_other)
        value_table = jnp.where(holds_keys, cache_other, cache_out)
        fresh_keys = jnp.where(holds_keys, fresh_mine[:, 0], fresh_other[:, 0])
        fresh_values = jnp.where(holds_keys, fresh_other[:, 0], fresh_mine[:, 0])
    else:
        key_table = cache_out[:, :HD]
        value_table = cache_out[:, HD:]
        fresh_keys = fresh_mine[:, 0]
        fresh_values = fresh_mine[:, 1]
    local_heads = query_sum.shape[1] // HD
    query_rot = rotate(query_sum.reshape(fresh_count, local_heads, HD), fresh_positions).astype(
        jnp.bfloat16
    )
    query_four = query_rot.reshape(NSEQ, STEPS, local_heads, HD)
    prefix_scores = (
        jnp.einsum(
            "sjhd,sld->sjhl",
            query_four,
            key_table.reshape(NSEQ, L, HD),
            preferred_element_type=jnp.float32,
        )
        * score_scale
    )
    live_keys = jnp.arange(L, dtype=jnp.int32)[None, :] < seq_lengths[:, None]
    prefix_scores = jnp.where(live_keys[:, None, None, :], prefix_scores, masked_score)
    fresh_scores = (
        jnp.einsum(
            "sjhd,sid->sjhi",
            query_four,
            fresh_keys.reshape(NSEQ, STEPS, HD),
            preferred_element_type=jnp.float32,
        )
        * score_scale
    )
    causal = jnp.arange(STEPS)[None, :] <= jnp.arange(STEPS)[:, None]
    fresh_scores = jnp.where(causal[None, :, None, :], fresh_scores, masked_score)
    row_max = jnp.maximum(jnp.max(prefix_scores, axis=-1), jnp.max(fresh_scores, axis=-1))
    prefix_weight = jnp.exp(prefix_scores - row_max[..., None])
    fresh_weight = jnp.exp(fresh_scores - row_max[..., None])
    denominator = jnp.sum(prefix_weight, axis=-1) + jnp.sum(fresh_weight, axis=-1)
    numerator = jnp.einsum(
        "sjhl,sld->sjhd",
        prefix_weight.astype(jnp.bfloat16),
        value_table.reshape(NSEQ, L, HD),
        preferred_element_type=jnp.float32,
    )
    numerator = numerator + jnp.einsum(
        "sjhi,sid->sjhd",
        fresh_weight.astype(jnp.bfloat16),
        fresh_values.reshape(NSEQ, STEPS, HD),
        preferred_element_type=jnp.float32,
    )
    attended = (
        (numerator / denominator[..., None])
        .reshape(fresh_count, local_heads * HD)
        .astype(jnp.bfloat16)
    )
    return (cache_out, project(attended, w_output, jnp.bfloat16, 1))


def solution(mesh):
    in_specs = (
        P("fsdp", "tp"),
        P("fsdp", "tp"),
        P("tp", "fsdp"),
        P("tp", "fsdp"),
        P("tp", "fsdp"),
        P("fsdp", None),
    )
    out_specs = (P("fsdp", "tp"), P("fsdp", "tp"))
    return jax.shard_map(body, mesh=mesh, in_specs=in_specs, out_specs=out_specs, check_vma=False)
```

```python
import functools

import jax
import jax.numpy as jnp
from jax import lax
from jax.experimental import pallas as pl
from jax.experimental.pallas import tpu as pltpu
from jax.sharding import PartitionSpec as P

HD = 128
NSEQ = 4
L = 1024
STEPS = 4
SKEW = 2
MESH = pl.DeviceIdType.MESH
VMEM = pl.BlockSpec(memory_space=pltpu.VMEM)


theta_base = 500000.0
masked_score = -1e30


def partner(block, axis, apart):
    count = lax.axis_size(axis)
    route = []
    for low in range(count):
        high = low | 1 << apart
        if high != low and high < count:
            route += [(low, high), (high, low)]
    return lax.ppermute(block, axis, route)


def rotate(values, positions):
    half_dim = values.shape[-1] // 2
    frequency = theta_base ** (-2.0 * jnp.arange(half_dim, dtype=jnp.float32) / values.shape[-1])
    angles = positions[:, None, None] * frequency[None, None, :]
    cosine = jnp.cos(angles)
    sine_part = jnp.sin(angles)
    lower_half = values[..., :half_dim]
    upper_half = values[..., half_dim:]
    return jnp.concatenate(
        [
            lower_half * cosine - upper_half * sine_part,
            upper_half * cosine + lower_half * sine_part,
        ],
        axis=-1,
    )


def flip(number, other, bits):
    result = 0
    for b in range(bits):
        one = lax.rem(lax.div(number, 1 << b), 2)
        two = lax.rem(lax.div(other, 1 << b), 2) if not isinstance(other, int) else (other >> b) & 1
        result = result + (one + two - 2 * one * two) * (1 << b)
    return result


def relay(f, t, groups, members, x_ref, x_all, near_out, near_in, far_in, sems):
    x_send, x_recv, near_send, near_recv, far_send, far_recv = sems
    rows = x_ref.shape[0]
    share = members // groups

    def across(j):
        return lax.rem(f + j, groups)

    def along(i):
        return lax.rem(t + i, members)

    def x_copy(j, slot):
        return pltpu.make_async_remote_copy(
            src_ref=x_ref, dst_ref=x_all.at[slot], send_sem=x_send.at[j], recv_sem=x_recv.at[slot],
            device_id=(across(j), t), device_id_type=MESH)

    def near_copy(j, slot):
        return pltpu.make_async_remote_copy(
            src_ref=near_out.at[:, pl.ds(pl.multiple_of(across(j) * rows, rows), rows)],
            dst_ref=near_in.at[slot], send_sem=near_send.at[j], recv_sem=near_recv.at[slot],
            device_id=(across(j), t), device_id_type=MESH)

    def far_copy(i, slot):
        to = along(i)
        return pltpu.make_async_remote_copy(
            src_ref=near_in.at[lax.div(to, share), lax.rem(to, share)],
            dst_ref=far_in.at[slot], send_sem=far_send.at[i], recv_sem=far_recv.at[slot],
            device_id=(f, to), device_id_type=MESH)

    def gather():
        for j in range(1, groups):
            x_copy(j, f).start()
        x_all[f] = x_ref[...]

    def multiply(weights):
        for j in range(1, groups):
            x_copy(j, across(j)).wait_recv()
        x = x_all[...].reshape(groups * rows, x_ref.shape[1])
        for h in range(share):
            base = 0
            for w_ref in weights:
                width = w_ref.shape[1] // share
                near_out[h, :, base:base + width] = jnp.dot(
                    x, w_ref[:, h * width:(h + 1) * width], preferred_element_type=jnp.float32
                ).astype(near_out.dtype)
                base += width
        for j in range(1, groups):
            near_copy(j, f).start()
        near_in[f] = near_out[:, pl.ds(pl.multiple_of(f * rows, rows), rows)]

    def scatter():
        for j in range(1, groups):
            near_copy(j, across(j)).wait_recv()
        for i in range(1, members):
            far_copy(i, t).start()
        far_in[t] = near_in[lax.div(t, share), lax.rem(t, share)]

    def collect():
        for i in range(1, members):
            far_copy(i, along(i)).wait_recv()
        result = far_in[0].astype(jnp.float32)
        for source in range(1, members):
            result += far_in[source].astype(jnp.float32)
        return result

    def drain():
        for j in range(1, groups):
            x_copy(j, f).wait_send()
            near_copy(j, f).wait_send()
        for i in range(1, members):
            far_copy(i, t).wait_send()

    return gather, multiply, scatter, collect, drain


def relay_scratch(groups, members, rows, depth, columns):
    share = members // groups
    return [
        pltpu.VMEM((groups, rows, depth), jnp.bfloat16),
        pltpu.VMEM((share, groups * rows, columns), jnp.bfloat16),
        pltpu.VMEM((groups, share, rows, columns), jnp.bfloat16),
        pltpu.VMEM((members, rows, columns), jnp.bfloat16),
    ] + [pltpu.SemaphoreType.DMA((n,)) for n in (groups, groups, groups, groups, members, members)]


def cache_kernel(groups, chips, pieces, x_ref, w_ref, cos_ref, sin_ref, new_ref, wq_ref,
                 out_ref, new_out_ref,
                 x_other, w_all, arrived, leaving, total,
                 x_send, x_recv, w_send, w_recv, sum_send, sum_recv,
                 new_all, near_out, near_in, far_in, *relay_sems):
    members = 2 * chips
    bits = (groups - 1).bit_length()
    f = lax.axis_index("fsdp")
    t = lax.axis_index("tp")
    c = lax.div(t, 2)
    e = lax.rem(t, 2)
    token_count = x_ref.shape[0]
    rows = token_count // pieces
    own = out_ref.shape[1]
    table_rows = cos_ref.shape[0]
    gather, multiply, scatter, collect, drain = relay(
        f, t, groups, members, new_ref, new_all, near_out, near_in, far_in, relay_sems)

    def piece(k):
        return pl.ds(pl.multiple_of(k * rows, rows), rows)

    def half(which):
        return pl.ds(pl.multiple_of(which * own, own), own)

    def x_copy(k):
        return pltpu.make_async_remote_copy(
            src_ref=x_ref.at[piece(k)], dst_ref=x_other.at[piece(k)],
            send_sem=x_send.at[k], recv_sem=x_recv.at[k],
            device_id=(f, 2 * c + 1 - e), device_id_type=MESH)

    def w_copy(j, swap):
        core = e if swap == 0 else 1 - e
        return pltpu.make_async_remote_copy(
            src_ref=w_ref.at[:, half(core)], dst_ref=w_all.at[j, swap],
            send_sem=w_send.at[j, swap], recv_sem=w_recv.at[j, swap],
            device_id=(flip(f, j, bits), 2 * c + core), device_id_type=MESH)

    def sum_copy(j, k, slot, chip):
        return pltpu.make_async_remote_copy(
            src_ref=leaving.at[j, piece(k)], dst_ref=arrived.at[slot, piece(k)],
            send_sem=sum_send.at[j, k], recv_sem=sum_recv.at[slot, k],
            device_id=(f, 2 * chip + e), device_id_type=MESH)

    def send_right(j, k):
        sum_copy(j, k, j, c + 1).start()

    def send_left(j, k, d):
        @pl.when(d == c - 1)
        def _():
            sum_copy(j, k, groups, c - 1).start()

        @pl.when(d < c - 1)
        def _():
            sum_copy(j, k, j, c - 1).start()

    def add_arrived(j, k):
        sum_copy(j, k, j, c).wait_recv()
        leaving[j, piece(k)] = (
            leaving[j, piece(k)].astype(jnp.float32) + arrived[j, piece(k)].astype(jnp.float32)
        ).astype(jnp.bfloat16)

    barrier = pltpu.get_barrier_semaphore()
    for j in range(1, groups):
        for core in range(2):
            pl.semaphore_signal(barrier, inc=1, device_id=(flip(f, j, bits), 2 * c + core),
                                device_id_type=MESH)
    for i in range(1, members):
        pl.semaphore_signal(barrier, inc=1, device_id=(f, lax.rem(t + i, members)),
                            device_id_type=MESH)
    pl.semaphore_wait(barrier, 2 * (groups - 1) + members - 1)

    w_copy(0, 1).start()
    for j in range(1, groups):
        for swap in range(2):
            w_copy(j, swap).start()

    @pl.loop(0, pieces)
    def _(k):
        x_copy(k).start()

    gather()
    w_all[0, 0] = w_ref[:, half(e)]
    w_copy(0, 1).wait_recv()

    @pl.loop(0, groups)
    def _(j):
        d = flip(f, j, bits)

        @pl.when(j == 1)
        def _():
            multiply([wq_ref, w_ref])

        @pl.when(j == groups - 1)
        def _():
            scatter()

        @pl.when(j > 0)
        def _():
            for swap in range(2):
                pltpu.make_async_remote_copy(
                    src_ref=w_ref.at[:, half(0)], dst_ref=w_all.at[j, swap],
                    send_sem=w_send.at[j, swap], recv_sem=w_recv.at[j, swap],
                    device_id=(f, 2 * c + 1 - e), device_id_type=MESH).wait_recv()

        @pl.loop(0, pieces)
        def _(k):
            @pl.when(j == 0)
            def _():
                x_copy(k).wait_recv()

            term = jnp.dot(x_ref[piece(k)], w_all[j, 0], preferred_element_type=jnp.float32)
            term += jnp.dot(x_other[piece(k)], w_all[j, 1], preferred_element_type=jnp.float32)

            @pl.when(d == c)
            def _():
                total[piece(k)] = term

            @pl.when(d != c)
            def _():
                leaving[j, piece(k)] = term.astype(jnp.bfloat16)

                @pl.when(c == 0)
                def _():
                    send_right(j, k)

                @pl.when(c == chips - 1)
                def _():
                    send_left(j, k, d)

    mine = flip(f, c, bits)
    from_right = flip(f, 0, bits)
    from_left = flip(f, chips - 1, bits)
    slot_right = mine - jnp.where(from_right < mine, 1, 0)
    slot_left = mine - jnp.where(from_left < mine, 1, 0)
    last = jnp.where(c == 0, slot_left, jnp.where(c == chips - 1, slot_right,
                                                  jnp.maximum(slot_left, slot_right)))

    def finish(k):
        @pl.when(c > 0)
        def _():
            sum_copy(mine, k, mine, c).wait_recv()
            total[piece(k)] += arrived[mine, piece(k)].astype(jnp.float32)

        @pl.when(c < chips - 1)
        def _():
            sum_copy(mine, k, groups, c).wait_recv()
            total[piece(k)] += arrived[groups, piece(k)].astype(jnp.float32)

        place = pl.ds(pl.multiple_of(lax.rem(k * rows, table_rows), rows), rows)
        for b in range(own // HD):
            cut = slice(b * HD, (b + 1) * HD)
            value = total[piece(k), cut]
            turned = value * cos_ref[place, cut] + pltpu.roll(value, HD // 2, 1) * sin_ref[place, cut]
            out_ref[piece(k), cut] = turned.astype(out_ref.dtype)

    count = (chips - 1) * pieces

    def at(step, distance):
        index = step - SKEW * distance
        known = jnp.minimum(jnp.maximum(index, 0), count - 1)
        valid = jnp.logical_and(index >= 0, index < count)
        return valid, lax.div(known, pieces), lax.rem(known, pieces)

    @pl.loop(0, count + SKEW * (chips - 1))
    def _(step):
        valid, slot, k_right = at(step, c)
        j_right = slot + jnp.where(from_right <= slot, 1, 0)
        d_right = flip(f, j_right, bits)

        @pl.when(jnp.logical_and(valid, jnp.logical_and(c > 0, d_right > c)))
        def _():
            add_arrived(j_right, k_right)
            send_right(j_right, k_right)

        valid, slot, k_left = at(step, chips - 1 - c)
        j_left = slot + jnp.where(from_left <= slot, 1, 0)
        d_left = flip(f, j_left, bits)

        @pl.when(jnp.logical_and(valid, jnp.logical_and(c < chips - 1, d_left < c)))
        def _():
            add_arrived(j_left, k_left)
            send_left(j_left, k_left, d_left)

        valid, slot, k_own = at(step, chips - 1)

        @pl.when(jnp.logical_and(valid, slot == last))
        def _():
            finish(k_own)

    new_out_ref[...] = collect()
    drain()
    w_copy(0, 1).wait_send()
    for j in range(1, groups):
        for swap in range(2):
            w_copy(j, swap).wait_send()

    @pl.loop(0, pieces)
    def _(k):
        x_copy(k).wait_send()

        @pl.loop(0, groups)
        def _(j):
            @pl.when(flip(f, j, bits) != c)
            def _():
                sum_copy(j, k, j, c).wait_send()


def recompute_cache(prefix_states, w_keyvalue, cosine, sine_part, new_states, w_query):
    groups, members = lax.axis_size("fsdp"), lax.axis_size("tp")
    chips = members // 2
    assert chips == groups and groups & (groups - 1) == 0
    token_count, depth = prefix_states.shape
    own = w_keyvalue.shape[1] // 2
    pieces = token_count // 256
    fresh_count = new_states.shape[0]
    fresh_width = (w_query.shape[1] + w_keyvalue.shape[1]) * groups // members
    return pl.pallas_call(
        functools.partial(cache_kernel, groups, chips, pieces),
        out_shape=(
            jax.ShapeDtypeStruct((token_count, own), jnp.bfloat16),
            jax.ShapeDtypeStruct((fresh_count, fresh_width), jnp.float32),
        ),
        in_specs=[VMEM] * 6,
        out_specs=(VMEM, VMEM),
        scratch_shapes=[
            pltpu.VMEM((token_count, depth), jnp.bfloat16),
            pltpu.VMEM((groups, 2, depth, own), jnp.bfloat16),
            pltpu.VMEM((groups + 1, token_count, own), jnp.bfloat16),
            pltpu.VMEM((groups, token_count, own), jnp.bfloat16),
            pltpu.VMEM((token_count, own), jnp.float32),
            pltpu.SemaphoreType.DMA((pieces,)),
            pltpu.SemaphoreType.DMA((pieces,)),
            pltpu.SemaphoreType.DMA((groups, 2)),
            pltpu.SemaphoreType.DMA((groups, 2)),
            pltpu.SemaphoreType.DMA((groups, pieces)),
            pltpu.SemaphoreType.DMA((groups + 1, pieces)),
        ] + relay_scratch(groups, members, fresh_count, depth, fresh_width),
        compiler_params=pltpu.CompilerParams(
            collective_id=0, has_side_effects=True, vmem_limit_bytes=60 * 1024 * 1024),
    )(prefix_states, w_keyvalue, cosine, sine_part, new_states, w_query)


def project_kernel(groups, members, x_ref, w_ref, out_ref, x_all, near_out, near_in, far_in, *sems):
    f = lax.axis_index("fsdp")
    t = lax.axis_index("tp")
    barrier = pltpu.get_barrier_semaphore()
    for j in range(1, groups):
        pl.semaphore_signal(barrier, inc=1, device_id=(lax.rem(f + j, groups), t),
                            device_id_type=MESH)
    for i in range(1, members):
        pl.semaphore_signal(barrier, inc=1, device_id=(f, lax.rem(t + i, members)),
                            device_id_type=MESH)
    pl.semaphore_wait(barrier, groups + members - 2)
    gather, multiply, scatter, collect, drain = relay(
        f, t, groups, members, x_ref, x_all, near_out, near_in, far_in, sems)
    gather()
    multiply([w_ref])
    scatter()
    out_ref[...] = collect().astype(out_ref.dtype)
    drain()


def project(x, weight, out_dtype, collective_id):
    groups, members = lax.axis_size("fsdp"), lax.axis_size("tp")
    rows, depth = x.shape
    columns = weight.shape[1] * groups // members
    return pl.pallas_call(
        functools.partial(project_kernel, groups, members),
        out_shape=jax.ShapeDtypeStruct((rows, columns), out_dtype),
        in_specs=[VMEM] * 2,
        out_specs=VMEM,
        scratch_shapes=relay_scratch(groups, members, rows, depth, columns),
        compiler_params=pltpu.CompilerParams(
            collective_id=collective_id, has_side_effects=True, vmem_limit_bytes=32 * 1024 * 1024),
    )(x, weight)


def body(prefix_states, new_states, w_query, w_keyvalue, w_output, lengths):
    my_index = lax.axis_index("tp")
    token_count = prefix_states.shape[0]
    fresh_count = new_states.shape[0]
    seq_lengths = lengths[0]
    score_scale = HD ** (-0.5)
    own_rows = w_keyvalue.shape[1] // 2
    block_count = own_rows // HD
    block_kind = (my_index * block_count + jnp.arange(block_count, dtype=jnp.int32)) % 2
    frequency = theta_base ** (-2.0 * jnp.arange(HD // 2, dtype=jnp.float32) / HD)
    angles = jnp.arange(L, dtype=jnp.int32).astype(jnp.float32)[:, None] * frequency[None, :]
    cosine, sine_part = jnp.cos(angles), jnp.sin(angles)
    is_key = jnp.repeat(block_kind == 0, HD)[None, :]
    cosine = jnp.where(is_key, jnp.tile(cosine, (1, 2 * block_count)), 1.0)
    sine_part = jnp.where(
        is_key, jnp.tile(jnp.concatenate([-sine_part, sine_part], axis=1), (1, block_count)), 0.0
    )
    cache_out, new_sum = recompute_cache(
        prefix_states, w_keyvalue, cosine, sine_part, new_states, w_query
    )
    query_width = new_sum.shape[1] - own_rows
    query_sum, fresh_sum = new_sum[:, :query_width], new_sum[:, query_width:]
    fresh_positions = (
        jnp.repeat(seq_lengths, STEPS) + jnp.tile(jnp.arange(STEPS, dtype=jnp.int32), NSEQ)
    ).astype(jnp.float32)
    fresh_blocks = fresh_sum.reshape(fresh_count, block_count, HD)
    fresh_rotated = rotate(fresh_blocks, fresh_positions)
    fresh_mine = jnp.where((block_kind == 0)[None, :, None], fresh_rotated, fresh_blocks).astype(
        jnp.bfloat16
    )
    if block_count == 1:
        cache_other, fresh_other = partner((cache_out, fresh_mine), "tp", 0)
        holds_keys = my_index % 2 == 0
        key_table = jnp.where(holds_keys, cache_out, cache_other)
        value_table = jnp.where(holds_keys, cache_other, cache_out)
        fresh_keys = jnp.where(holds_keys, fresh_mine[:, 0], fresh_other[:, 0])
        fresh_values = jnp.where(holds_keys, fresh_other[:, 0], fresh_mine[:, 0])
    else:
        key_table = cache_out[:, :HD]
        value_table = cache_out[:, HD:]
        fresh_keys = fresh_mine[:, 0]
        fresh_values = fresh_mine[:, 1]
    local_heads = query_sum.shape[1] // HD
    query_rot = rotate(query_sum.reshape(fresh_count, local_heads, HD), fresh_positions).astype(
        jnp.bfloat16
    )
    query_four = query_rot.reshape(NSEQ, STEPS, local_heads, HD)
    prefix_scores = (
        jnp.einsum(
            "sjhd,sld->sjhl",
            query_four,
            key_table.reshape(NSEQ, L, HD),
            preferred_element_type=jnp.float32,
        )
        * score_scale
    )
    live_keys = jnp.arange(L, dtype=jnp.int32)[None, :] < seq_lengths[:, None]
    prefix_scores = jnp.where(live_keys[:, None, None, :], prefix_scores, masked_score)
    fresh_scores = (
        jnp.einsum(
            "sjhd,sid->sjhi",
            query_four,
            fresh_keys.reshape(NSEQ, STEPS, HD),
            preferred_element_type=jnp.float32,
        )
        * score_scale
    )
    causal = jnp.arange(STEPS)[None, :] <= jnp.arange(STEPS)[:, None]
    fresh_scores = jnp.where(causal[None, :, None, :], fresh_scores, masked_score)
    row_max = jnp.maximum(jnp.max(prefix_scores, axis=-1), jnp.max(fresh_scores, axis=-1))
    prefix_weight = jnp.exp(prefix_scores - row_max[..., None])
    fresh_weight = jnp.exp(fresh_scores - row_max[..., None])
    denominator = jnp.sum(prefix_weight, axis=-1) + jnp.sum(fresh_weight, axis=-1)
    numerator = jnp.einsum(
        "sjhl,sld->sjhd",
        prefix_weight.astype(jnp.bfloat16),
        value_table.reshape(NSEQ, L, HD),
        preferred_element_type=jnp.float32,
    )
    numerator = numerator + jnp.einsum(
        "sjhi,sid->sjhd",
        fresh_weight.astype(jnp.bfloat16),
        fresh_values.reshape(NSEQ, STEPS, HD),
        preferred_element_type=jnp.float32,
    )
    attended = (
        (numerator / denominator[..., None])
        .reshape(fresh_count, local_heads * HD)
        .astype(jnp.bfloat16)
    )
    return (cache_out, project(attended, w_output, jnp.bfloat16, 1))


def solution(mesh):
    in_specs = (
        P("fsdp", "tp"),
        P("fsdp", "tp"),
        P("tp", "fsdp"),
        P("tp", "fsdp"),
        P("tp", "fsdp"),
        P("fsdp", None),
    )
    out_specs = (P("fsdp", "tp"), P("fsdp", "tp"))
    return jax.shard_map(body, mesh=mesh, in_specs=in_specs, out_specs=out_specs, check_vma=False)
```

```python
import functools

import jax
import jax.numpy as jnp
from jax import lax
from jax.experimental import pallas as pl
from jax.experimental.pallas import tpu as pltpu
from jax.sharding import PartitionSpec as P

HD = 128
NSEQ = 4
L = 1024
STEPS = 4
SKEW = 2
MESH = pl.DeviceIdType.MESH
VMEM = pl.BlockSpec(memory_space=pltpu.VMEM)


theta_base = 500000.0
masked_score = -1e30


def partner(block, axis, apart):
    count = lax.axis_size(axis)
    route = []
    for low in range(count):
        high = low | 1 << apart
        if high != low and high < count:
            route += [(low, high), (high, low)]
    return lax.ppermute(block, axis, route)


def rotate(values, positions):
    half_dim = values.shape[-1] // 2
    frequency = theta_base ** (-2.0 * jnp.arange(half_dim, dtype=jnp.float32) / values.shape[-1])
    angles = positions[:, None, None] * frequency[None, None, :]
    cosine = jnp.cos(angles)
    sine_part = jnp.sin(angles)
    lower_half = values[..., :half_dim]
    upper_half = values[..., half_dim:]
    return jnp.concatenate(
        [
            lower_half * cosine - upper_half * sine_part,
            upper_half * cosine + lower_half * sine_part,
        ],
        axis=-1,
    )


def flip(number, other, bits):
    result = 0
    for b in range(bits):
        one = lax.rem(lax.div(number, 1 << b), 2)
        two = lax.rem(lax.div(other, 1 << b), 2) if not isinstance(other, int) else (other >> b) & 1
        result = result + (one + two - 2 * one * two) * (1 << b)
    return result


def relay(f, t, groups, members, x_ref, x_all, near_out, near_in, far_in, sems):
    x_send, x_recv, near_send, near_recv, far_send, far_recv = sems
    rows = x_ref.shape[0]
    share = members // groups

    def across(j):
        return lax.rem(f + j, groups)

    def along(i):
        return lax.rem(t + i, members)

    def x_copy(j, slot):
        return pltpu.make_async_remote_copy(
            src_ref=x_ref, dst_ref=x_all.at[slot], send_sem=x_send.at[j], recv_sem=x_recv.at[slot],
            device_id=(across(j), t), device_id_type=MESH)

    def near_copy(j, slot):
        return pltpu.make_async_remote_copy(
            src_ref=near_out.at[:, pl.ds(pl.multiple_of(across(j) * rows, rows), rows)],
            dst_ref=near_in.at[slot], send_sem=near_send.at[j], recv_sem=near_recv.at[slot],
            device_id=(across(j), t), device_id_type=MESH)

    def far_copy(i, slot):
        to = along(i)
        return pltpu.make_async_remote_copy(
            src_ref=near_in.at[lax.div(to, share), lax.rem(to, share)],
            dst_ref=far_in.at[slot], send_sem=far_send.at[i], recv_sem=far_recv.at[slot],
            device_id=(f, to), device_id_type=MESH)

    def gather():
        for j in range(1, groups):
            x_copy(j, f).start()
        x_all[f] = x_ref[...]

    def multiply(weights):
        for j in range(1, groups):
            x_copy(j, across(j)).wait_recv()
        x = x_all[...].reshape(groups * rows, x_ref.shape[1])
        for h in range(share):
            base = 0
            for w_ref in weights:
                width = w_ref.shape[1] // share
                near_out[h, :, base:base + width] = jnp.dot(
                    x, w_ref[:, h * width:(h + 1) * width], preferred_element_type=jnp.float32
                ).astype(near_out.dtype)
                base += width
        for j in range(1, groups):
            near_copy(j, f).start()
        near_in[f] = near_out[:, pl.ds(pl.multiple_of(f * rows, rows), rows)]

    def scatter():
        for j in range(1, groups):
            near_copy(j, across(j)).wait_recv()
        for i in range(1, members):
            far_copy(i, t).start()
        far_in[t] = near_in[lax.div(t, share), lax.rem(t, share)]

    def collect():
        for i in range(1, members):
            far_copy(i, along(i)).wait_recv()
        result = far_in[0].astype(jnp.float32)
        for source in range(1, members):
            result += far_in[source].astype(jnp.float32)
        return result

    def drain():
        for j in range(1, groups):
            x_copy(j, f).wait_send()
            near_copy(j, f).wait_send()
        for i in range(1, members):
            far_copy(i, t).wait_send()

    return gather, multiply, scatter, collect, drain


def relay_scratch(groups, members, rows, depth, columns):
    share = members // groups
    return [
        pltpu.VMEM((groups, rows, depth), jnp.bfloat16),
        pltpu.VMEM((share, groups * rows, columns), jnp.bfloat16),
        pltpu.VMEM((groups, share, rows, columns), jnp.bfloat16),
        pltpu.VMEM((members, rows, columns), jnp.bfloat16),
    ] + [pltpu.SemaphoreType.DMA((n,)) for n in (groups, groups, groups, groups, members, members)]


def cache_kernel(groups, chips, pieces, x_ref, w_ref, cos_ref, sin_ref, new_ref, wq_ref,
                 out_ref, new_out_ref,
                 x_other, w_all, arrived, leaving, total,
                 x_send, x_recv, w_send, w_recv, sum_send, sum_recv,
                 new_all, near_out, near_in, far_in, *relay_sems):
    members = 2 * chips
    bits = (groups - 1).bit_length()
    f = lax.axis_index("fsdp")
    t = lax.axis_index("tp")
    c = lax.div(t, 2)
    e = lax.rem(t, 2)
    token_count = x_ref.shape[0]
    rows = token_count // pieces
    own = out_ref.shape[1]
    table_rows = cos_ref.shape[0]
    gather, multiply, scatter, collect, drain = relay(
        f, t, groups, members, new_ref, new_all, near_out, near_in, far_in, relay_sems)

    def piece(k):
        return pl.ds(pl.multiple_of(k * rows, rows), rows)

    def half(which):
        return pl.ds(pl.multiple_of(which * own, own), own)

    def x_copy(k):
        return pltpu.make_async_remote_copy(
            src_ref=x_ref.at[piece(k)], dst_ref=x_other.at[piece(k)],
            send_sem=x_send.at[k], recv_sem=x_recv.at[k],
            device_id=(f, 2 * c + 1 - e), device_id_type=MESH)

    def w_copy(j, swap):
        core = e if swap == 0 else 1 - e
        return pltpu.make_async_remote_copy(
            src_ref=w_ref.at[:, half(core)], dst_ref=w_all.at[j, swap],
            send_sem=w_send.at[j, swap], recv_sem=w_recv.at[j, swap],
            device_id=(flip(f, j, bits), 2 * c + core), device_id_type=MESH)

    def sum_copy(j, k, slot, chip):
        return pltpu.make_async_remote_copy(
            src_ref=leaving.at[j, piece(k)], dst_ref=arrived.at[slot, piece(k)],
            send_sem=sum_send.at[j, k], recv_sem=sum_recv.at[slot, k],
            device_id=(f, 2 * chip + e), device_id_type=MESH)

    def send_right(j, k):
        sum_copy(j, k, j, c + 1).start()

    def send_left(j, k, d):
        @pl.when(d == c - 1)
        def _():
            sum_copy(j, k, groups, c - 1).start()

        @pl.when(d < c - 1)
        def _():
            sum_copy(j, k, j, c - 1).start()

    def add_arrived(j, k):
        sum_copy(j, k, j, c).wait_recv()
        leaving[j, piece(k)] = (
            leaving[j, piece(k)].astype(jnp.float32) + arrived[j, piece(k)].astype(jnp.float32)
        ).astype(jnp.bfloat16)

    barrier = pltpu.get_barrier_semaphore()
    for j in range(1, groups):
        for core in range(2):
            pl.semaphore_signal(barrier, inc=1, device_id=(flip(f, j, bits), 2 * c + core),
                                device_id_type=MESH)
    for i in range(1, members):
        pl.semaphore_signal(barrier, inc=1, device_id=(f, lax.rem(t + i, members)),
                            device_id_type=MESH)
    pl.semaphore_wait(barrier, 2 * (groups - 1) + members - 1)

    direct = [j for j in range(1, groups) if j & (j - 1) == 0]
    w_copy(0, 1).start()
    for j in direct:
        for swap in range(2):
            w_copy(j, swap).start()

    @pl.loop(0, pieces)
    def _(k):
        x_copy(k).start()

    gather()
    w_all[0, 0] = w_ref[:, half(e)]
    w_copy(0, 1).wait_recv()

    @pl.loop(0, groups)
    def _(j):
        d = flip(f, j, bits)

        @pl.when(j == 1)
        def _():
            multiply([wq_ref, w_ref])

        @pl.when(j == groups - 1)
        def _():
            scatter()

        @pl.when(j > 0)
        def _():
            for swap in range(2):
                pltpu.make_async_remote_copy(
                    src_ref=w_ref.at[:, half(0)], dst_ref=w_all.at[j, swap],
                    send_sem=w_send.at[j, swap], recv_sem=w_recv.at[j, swap],
                    device_id=(f, 2 * c + 1 - e), device_id_type=MESH).wait_recv()

        @pl.when(j == 1)
        def _():
            for later in range(1, groups):
                if later not in direct:
                    for swap in range(2):
                        w_copy(later, swap).start()

        @pl.loop(0, pieces)
        def _(k):
            @pl.when(j == 0)
            def _():
                x_copy(k).wait_recv()

            term = jnp.dot(x_ref[piece(k)], w_all[j, 0], preferred_element_type=jnp.float32)
            term += jnp.dot(x_other[piece(k)], w_all[j, 1], preferred_element_type=jnp.float32)

            @pl.when(d == c)
            def _():
                total[piece(k)] = term

            @pl.when(d != c)
            def _():
                leaving[j, piece(k)] = term.astype(jnp.bfloat16)

                @pl.when(c == 0)
                def _():
                    send_right(j, k)

                @pl.when(c == chips - 1)
                def _():
                    send_left(j, k, d)

    mine = flip(f, c, bits)
    from_right = flip(f, 0, bits)
    from_left = flip(f, chips - 1, bits)
    slot_right = mine - jnp.where(from_right < mine, 1, 0)
    slot_left = mine - jnp.where(from_left < mine, 1, 0)
    last = jnp.where(c == 0, slot_left, jnp.where(c == chips - 1, slot_right,
                                                  jnp.maximum(slot_left, slot_right)))

    def finish(k):
        @pl.when(c > 0)
        def _():
            sum_copy(mine, k, mine, c).wait_recv()
            total[piece(k)] += arrived[mine, piece(k)].astype(jnp.float32)

        @pl.when(c < chips - 1)
        def _():
            sum_copy(mine, k, groups, c).wait_recv()
            total[piece(k)] += arrived[groups, piece(k)].astype(jnp.float32)

        place = pl.ds(pl.multiple_of(lax.rem(k * rows, table_rows), rows), rows)
        for b in range(own // HD):
            cut = slice(b * HD, (b + 1) * HD)
            value = total[piece(k), cut]
            turned = value * cos_ref[place, cut] + pltpu.roll(value, HD // 2, 1) * sin_ref[place, cut]
            out_ref[piece(k), cut] = turned.astype(out_ref.dtype)

    count = (chips - 1) * pieces

    def at(step, distance):
        index = step - SKEW * distance
        known = jnp.minimum(jnp.maximum(index, 0), count - 1)
        valid = jnp.logical_and(index >= 0, index < count)
        return valid, lax.div(known, pieces), lax.rem(known, pieces)

    @pl.loop(0, count + SKEW * (chips - 1))
    def _(step):
        valid, slot, k_right = at(step, c)
        j_right = slot + jnp.where(from_right <= slot, 1, 0)
        d_right = flip(f, j_right, bits)

        @pl.when(jnp.logical_and(valid, jnp.logical_and(c > 0, d_right > c)))
        def _():
            add_arrived(j_right, k_right)
            send_right(j_right, k_right)

        valid, slot, k_left = at(step, chips - 1 - c)
        j_left = slot + jnp.where(from_left <= slot, 1, 0)
        d_left = flip(f, j_left, bits)

        @pl.when(jnp.logical_and(valid, jnp.logical_and(c < chips - 1, d_left < c)))
        def _():
            add_arrived(j_left, k_left)
            send_left(j_left, k_left, d_left)

        valid, slot, k_own = at(step, chips - 1)

        @pl.when(jnp.logical_and(valid, slot == last))
        def _():
            finish(k_own)

    new_out_ref[...] = collect()
    drain()
    w_copy(0, 1).wait_send()
    for j in range(1, groups):
        for swap in range(2):
            w_copy(j, swap).wait_send()

    @pl.loop(0, pieces)
    def _(k):
        x_copy(k).wait_send()

        @pl.loop(0, groups)
        def _(j):
            @pl.when(flip(f, j, bits) != c)
            def _():
                sum_copy(j, k, j, c).wait_send()


def recompute_cache(prefix_states, w_keyvalue, cosine, sine_part, new_states, w_query):
    groups, members = lax.axis_size("fsdp"), lax.axis_size("tp")
    chips = members // 2
    assert chips == groups and groups & (groups - 1) == 0
    token_count, depth = prefix_states.shape
    own = w_keyvalue.shape[1] // 2
    pieces = token_count // 256
    fresh_count = new_states.shape[0]
    fresh_width = (w_query.shape[1] + w_keyvalue.shape[1]) * groups // members
    return pl.pallas_call(
        functools.partial(cache_kernel, groups, chips, pieces),
        out_shape=(
            jax.ShapeDtypeStruct((token_count, own), jnp.bfloat16),
            jax.ShapeDtypeStruct((fresh_count, fresh_width), jnp.float32),
        ),
        in_specs=[VMEM] * 6,
        out_specs=(VMEM, VMEM),
        scratch_shapes=[
            pltpu.VMEM((token_count, depth), jnp.bfloat16),
            pltpu.VMEM((groups, 2, depth, own), jnp.bfloat16),
            pltpu.VMEM((groups + 1, token_count, own), jnp.bfloat16),
            pltpu.VMEM((groups, token_count, own), jnp.bfloat16),
            pltpu.VMEM((token_count, own), jnp.float32),
            pltpu.SemaphoreType.DMA((pieces,)),
            pltpu.SemaphoreType.DMA((pieces,)),
            pltpu.SemaphoreType.DMA((groups, 2)),
            pltpu.SemaphoreType.DMA((groups, 2)),
            pltpu.SemaphoreType.DMA((groups, pieces)),
            pltpu.SemaphoreType.DMA((groups + 1, pieces)),
        ] + relay_scratch(groups, members, fresh_count, depth, fresh_width),
        compiler_params=pltpu.CompilerParams(
            collective_id=0, has_side_effects=True, vmem_limit_bytes=60 * 1024 * 1024),
    )(prefix_states, w_keyvalue, cosine, sine_part, new_states, w_query)


def project_kernel(groups, members, x_ref, w_ref, out_ref, x_all, near_out, near_in, far_in, *sems):
    f = lax.axis_index("fsdp")
    t = lax.axis_index("tp")
    barrier = pltpu.get_barrier_semaphore()
    for j in range(1, groups):
        pl.semaphore_signal(barrier, inc=1, device_id=(lax.rem(f + j, groups), t),
                            device_id_type=MESH)
    for i in range(1, members):
        pl.semaphore_signal(barrier, inc=1, device_id=(f, lax.rem(t + i, members)),
                            device_id_type=MESH)
    pl.semaphore_wait(barrier, groups + members - 2)
    gather, multiply, scatter, collect, drain = relay(
        f, t, groups, members, x_ref, x_all, near_out, near_in, far_in, sems)
    gather()
    multiply([w_ref])
    scatter()
    out_ref[...] = collect().astype(out_ref.dtype)
    drain()


def project(x, weight, out_dtype, collective_id):
    groups, members = lax.axis_size("fsdp"), lax.axis_size("tp")
    rows, depth = x.shape
    columns = weight.shape[1] * groups // members
    return pl.pallas_call(
        functools.partial(project_kernel, groups, members),
        out_shape=jax.ShapeDtypeStruct((rows, columns), out_dtype),
        in_specs=[VMEM] * 2,
        out_specs=VMEM,
        scratch_shapes=relay_scratch(groups, members, rows, depth, columns),
        compiler_params=pltpu.CompilerParams(
            collective_id=collective_id, has_side_effects=True, vmem_limit_bytes=32 * 1024 * 1024),
    )(x, weight)


def body(prefix_states, new_states, w_query, w_keyvalue, w_output, lengths):
    my_index = lax.axis_index("tp")
    token_count = prefix_states.shape[0]
    fresh_count = new_states.shape[0]
    seq_lengths = lengths[0]
    score_scale = HD ** (-0.5)
    own_rows = w_keyvalue.shape[1] // 2
    block_count = own_rows // HD
    block_kind = (my_index * block_count + jnp.arange(block_count, dtype=jnp.int32)) % 2
    frequency = theta_base ** (-2.0 * jnp.arange(HD // 2, dtype=jnp.float32) / HD)
    angles = jnp.arange(L, dtype=jnp.int32).astype(jnp.float32)[:, None] * frequency[None, :]
    cosine, sine_part = jnp.cos(angles), jnp.sin(angles)
    is_key = jnp.repeat(block_kind == 0, HD)[None, :]
    cosine = jnp.where(is_key, jnp.tile(cosine, (1, 2 * block_count)), 1.0)
    sine_part = jnp.where(
        is_key, jnp.tile(jnp.concatenate([-sine_part, sine_part], axis=1), (1, block_count)), 0.0
    )
    cache_out, new_sum = recompute_cache(
        prefix_states, w_keyvalue, cosine, sine_part, new_states, w_query
    )
    query_width = new_sum.shape[1] - own_rows
    query_sum, fresh_sum = new_sum[:, :query_width], new_sum[:, query_width:]
    fresh_positions = (
        jnp.repeat(seq_lengths, STEPS) + jnp.tile(jnp.arange(STEPS, dtype=jnp.int32), NSEQ)
    ).astype(jnp.float32)
    fresh_blocks = fresh_sum.reshape(fresh_count, block_count, HD)
    fresh_rotated = rotate(fresh_blocks, fresh_positions)
    fresh_mine = jnp.where((block_kind == 0)[None, :, None], fresh_rotated, fresh_blocks).astype(
        jnp.bfloat16
    )
    if block_count == 1:
        cache_other, fresh_other = partner((cache_out, fresh_mine), "tp", 0)
        holds_keys = my_index % 2 == 0
        key_table = jnp.where(holds_keys, cache_out, cache_other)
        value_table = jnp.where(holds_keys, cache_other, cache_out)
        fresh_keys = jnp.where(holds_keys, fresh_mine[:, 0], fresh_other[:, 0])
        fresh_values = jnp.where(holds_keys, fresh_other[:, 0], fresh_mine[:, 0])
    else:
        key_table = cache_out[:, :HD]
        value_table = cache_out[:, HD:]
        fresh_keys = fresh_mine[:, 0]
        fresh_values = fresh_mine[:, 1]
    local_heads = query_sum.shape[1] // HD
    query_rot = rotate(query_sum.reshape(fresh_count, local_heads, HD), fresh_positions).astype(
        jnp.bfloat16
    )
    query_four = query_rot.reshape(NSEQ, STEPS, local_heads, HD)
    prefix_scores = (
        jnp.einsum(
            "sjhd,sld->sjhl",
            query_four,
            key_table.reshape(NSEQ, L, HD),
            preferred_element_type=jnp.float32,
        )
        * score_scale
    )
    live_keys = jnp.arange(L, dtype=jnp.int32)[None, :] < seq_lengths[:, None]
    prefix_scores = jnp.where(live_keys[:, None, None, :], prefix_scores, masked_score)
    fresh_scores = (
        jnp.einsum(
            "sjhd,sid->sjhi",
            query_four,
            fresh_keys.reshape(NSEQ, STEPS, HD),
            preferred_element_type=jnp.float32,
        )
        * score_scale
    )
    causal = jnp.arange(STEPS)[None, :] <= jnp.arange(STEPS)[:, None]
    fresh_scores = jnp.where(causal[None, :, None, :], fresh_scores, masked_score)
    row_max = jnp.maximum(jnp.max(prefix_scores, axis=-1), jnp.max(fresh_scores, axis=-1))
    prefix_weight = jnp.exp(prefix_scores - row_max[..., None])
    fresh_weight = jnp.exp(fresh_scores - row_max[..., None])
    denominator = jnp.sum(prefix_weight, axis=-1) + jnp.sum(fresh_weight, axis=-1)
    numerator = jnp.einsum(
        "sjhl,sld->sjhd",
        prefix_weight.astype(jnp.bfloat16),
        value_table.reshape(NSEQ, L, HD),
        preferred_element_type=jnp.float32,
    )
    numerator = numerator + jnp.einsum(
        "sjhi,sid->sjhd",
        fresh_weight.astype(jnp.bfloat16),
        fresh_values.reshape(NSEQ, STEPS, HD),
        preferred_element_type=jnp.float32,
    )
    attended = (
        (numerator / denominator[..., None])
        .reshape(fresh_count, local_heads * HD)
        .astype(jnp.bfloat16)
    )
    return (cache_out, project(attended, w_output, jnp.bfloat16, 1))


def solution(mesh):
    in_specs = (
        P("fsdp", "tp"),
        P("fsdp", "tp"),
        P("tp", "fsdp"),
        P("tp", "fsdp"),
        P("tp", "fsdp"),
        P("fsdp", None),
    )
    out_specs = (P("fsdp", "tp"), P("fsdp", "tp"))
    return jax.shard_map(body, mesh=mesh, in_specs=in_specs, out_specs=out_specs, check_vma=False)
```

```python
import functools

import jax
import jax.numpy as jnp
from jax import lax
from jax.experimental import pallas as pl
from jax.experimental.pallas import tpu as pltpu
from jax.sharding import PartitionSpec as P

HD = 128
NSEQ = 4
L = 1024
STEPS = 4
SKEW = 2
WINDOW = 3
MESH = pl.DeviceIdType.MESH
VMEM = pl.BlockSpec(memory_space=pltpu.VMEM)


theta_base = 500000.0
masked_score = -1e30


def partner(block, axis, apart):
    count = lax.axis_size(axis)
    route = []
    for low in range(count):
        high = low | 1 << apart
        if high != low and high < count:
            route += [(low, high), (high, low)]
    return lax.ppermute(block, axis, route)


def rotate(values, positions):
    half_dim = values.shape[-1] // 2
    frequency = theta_base ** (-2.0 * jnp.arange(half_dim, dtype=jnp.float32) / values.shape[-1])
    angles = positions[:, None, None] * frequency[None, None, :]
    cosine = jnp.cos(angles)
    sine_part = jnp.sin(angles)
    lower_half = values[..., :half_dim]
    upper_half = values[..., half_dim:]
    return jnp.concatenate(
        [
            lower_half * cosine - upper_half * sine_part,
            upper_half * cosine + lower_half * sine_part,
        ],
        axis=-1,
    )


def flip(number, other, bits):
    result = 0
    for b in range(bits):
        one = lax.rem(lax.div(number, 1 << b), 2)
        two = lax.rem(lax.div(other, 1 << b), 2) if not isinstance(other, int) else (other >> b) & 1
        result = result + (one + two - 2 * one * two) * (1 << b)
    return result


def relay(f, t, groups, members, x_ref, x_all, near_out, near_in, far_in, sems):
    x_send, x_recv, near_send, near_recv, far_send, far_recv = sems
    rows = x_ref.shape[0]
    share = members // groups

    def across(j):
        return lax.rem(f + j, groups)

    def along(i):
        return lax.rem(t + i, members)

    def x_copy(j, slot):
        return pltpu.make_async_remote_copy(
            src_ref=x_ref, dst_ref=x_all.at[slot], send_sem=x_send.at[j], recv_sem=x_recv.at[slot],
            device_id=(across(j), t), device_id_type=MESH)

    def near_copy(j, slot):
        return pltpu.make_async_remote_copy(
            src_ref=near_out.at[:, pl.ds(pl.multiple_of(across(j) * rows, rows), rows)],
            dst_ref=near_in.at[slot], send_sem=near_send.at[j], recv_sem=near_recv.at[slot],
            device_id=(across(j), t), device_id_type=MESH)

    def far_copy(i, slot):
        to = along(i)
        return pltpu.make_async_remote_copy(
            src_ref=near_in.at[lax.div(to, share), lax.rem(to, share)],
            dst_ref=far_in.at[slot], send_sem=far_send.at[i], recv_sem=far_recv.at[slot],
            device_id=(f, to), device_id_type=MESH)

    def gather():
        for j in range(1, groups):
            x_copy(j, f).start()
        x_all[f] = x_ref[...]

    def multiply(weights):
        for j in range(1, groups):
            x_copy(j, across(j)).wait_recv()
        x = x_all[...].reshape(groups * rows, x_ref.shape[1])
        for h in range(share):
            base = 0
            for w_ref in weights:
                width = w_ref.shape[1] // share
                near_out[h, :, base:base + width] = jnp.dot(
                    x, w_ref[:, h * width:(h + 1) * width], preferred_element_type=jnp.float32
                ).astype(near_out.dtype)
                base += width
        for j in range(1, groups):
            near_copy(j, f).start()
        near_in[f] = near_out[:, pl.ds(pl.multiple_of(f * rows, rows), rows)]

    def scatter():
        for j in range(1, groups):
            near_copy(j, across(j)).wait_recv()
        for i in range(1, members):
            far_copy(i, t).start()
        far_in[t] = near_in[lax.div(t, share), lax.rem(t, share)]

    def collect():
        for i in range(1, members):
            far_copy(i, along(i)).wait_recv()
        result = far_in[0].astype(jnp.float32)
        for source in range(1, members):
            result += far_in[source].astype(jnp.float32)
        return result

    def drain():
        for j in range(1, groups):
            x_copy(j, f).wait_send()
            near_copy(j, f).wait_send()
        for i in range(1, members):
            far_copy(i, t).wait_send()

    return gather, multiply, scatter, collect, drain


def relay_scratch(groups, members, rows, depth, columns):
    share = members // groups
    return [
        pltpu.VMEM((groups, rows, depth), jnp.bfloat16),
        pltpu.VMEM((share, groups * rows, columns), jnp.bfloat16),
        pltpu.VMEM((groups, share, rows, columns), jnp.bfloat16),
        pltpu.VMEM((members, rows, columns), jnp.bfloat16),
    ] + [pltpu.SemaphoreType.DMA((n,)) for n in (groups, groups, groups, groups, members, members)]


def cache_kernel(groups, chips, pieces, x_ref, w_ref, cos_ref, sin_ref, new_ref, wq_ref,
                 out_ref, new_out_ref,
                 x_other, w_all, arrived, leaving, total,
                 x_send, x_recv, w_send, w_recv, sum_send, sum_recv,
                 new_all, near_out, near_in, far_in, *relay_sems):
    members = 2 * chips
    bits = (groups - 1).bit_length()
    f = lax.axis_index("fsdp")
    t = lax.axis_index("tp")
    c = lax.div(t, 2)
    e = lax.rem(t, 2)
    token_count = x_ref.shape[0]
    rows = token_count // pieces
    own = out_ref.shape[1]
    table_rows = cos_ref.shape[0]
    gather, multiply, scatter, collect, drain = relay(
        f, t, groups, members, new_ref, new_all, near_out, near_in, far_in, relay_sems)

    def piece(k):
        return pl.ds(pl.multiple_of(k * rows, rows), rows)

    def half(which):
        return pl.ds(pl.multiple_of(which * own, own), own)

    def x_copy(k):
        return pltpu.make_async_remote_copy(
            src_ref=x_ref.at[piece(k)], dst_ref=x_other.at[piece(k)],
            send_sem=x_send.at[k], recv_sem=x_recv.at[k],
            device_id=(f, 2 * c + 1 - e), device_id_type=MESH)

    def w_copy(j, swap):
        core = e if swap == 0 else 1 - e
        return pltpu.make_async_remote_copy(
            src_ref=w_ref.at[:, half(core)], dst_ref=w_all.at[j, swap],
            send_sem=w_send.at[j, swap], recv_sem=w_recv.at[j, swap],
            device_id=(flip(f, j, bits), 2 * c + core), device_id_type=MESH)

    def sum_copy(j, k, slot, chip):
        return pltpu.make_async_remote_copy(
            src_ref=leaving.at[j, piece(k)], dst_ref=arrived.at[slot, piece(k)],
            send_sem=sum_send.at[j, k], recv_sem=sum_recv.at[slot, k],
            device_id=(f, 2 * chip + e), device_id_type=MESH)

    def send_right(j, k):
        sum_copy(j, k, j, c + 1).start()

    def send_left(j, k, d):
        @pl.when(d == c - 1)
        def _():
            sum_copy(j, k, groups, c - 1).start()

        @pl.when(d < c - 1)
        def _():
            sum_copy(j, k, j, c - 1).start()

    def add_arrived(j, k):
        sum_copy(j, k, j, c).wait_recv()
        leaving[j, piece(k)] = (
            leaving[j, piece(k)].astype(jnp.float32) + arrived[j, piece(k)].astype(jnp.float32)
        ).astype(jnp.bfloat16)

    barrier = pltpu.get_barrier_semaphore()
    for j in range(1, groups):
        for core in range(2):
            pl.semaphore_signal(barrier, inc=1, device_id=(flip(f, j, bits), 2 * c + core),
                                device_id_type=MESH)
    for i in range(1, members):
        pl.semaphore_signal(barrier, inc=1, device_id=(f, lax.rem(t + i, members)),
                            device_id_type=MESH)
    pl.semaphore_wait(barrier, 2 * (groups - 1) + members - 1)

    direct = [j for j in range(1, groups) if j & (j - 1) == 0]
    w_copy(0, 1).start()
    for j in direct:
        for swap in range(2):
            w_copy(j, swap).start()

    @pl.loop(0, pieces)
    def _(k):
        x_copy(k).start()

    gather()
    at_end = jnp.logical_or(c == 0, c == chips - 1)
    omitted = jnp.where(c == 0, flip(f, 0, bits), flip(f, chips - 1, bits))
    w_all[0, 0] = w_ref[:, half(e)]
    w_copy(0, 1).wait_recv()

    @pl.loop(0, groups)
    def _(j):
        d = flip(f, j, bits)

        @pl.when(j == 1)
        def _():
            multiply([wq_ref, w_ref])

        @pl.when(j == groups - 1)
        def _():
            scatter()

        @pl.when(j > 0)
        def _():
            for swap in range(2):
                pltpu.make_async_remote_copy(
                    src_ref=w_ref.at[:, half(0)], dst_ref=w_all.at[j, swap],
                    send_sem=w_send.at[j, swap], recv_sem=w_recv.at[j, swap],
                    device_id=(f, 2 * c + 1 - e), device_id_type=MESH).wait_recv()

        @pl.when(j == 1)
        def _():
            for later in range(1, groups):
                if later not in direct:
                    for swap in range(2):
                        w_copy(later, swap).start()

        @pl.loop(0, pieces)
        def _(k):
            @pl.when(j == 0)
            def _():
                x_copy(k).wait_recv()

            term = jnp.dot(x_ref[piece(k)], w_all[j, 0], preferred_element_type=jnp.float32)
            term += jnp.dot(x_other[piece(k)], w_all[j, 1], preferred_element_type=jnp.float32)

            @pl.when(d == c)
            def _():
                total[piece(k)] = term

            @pl.when(d != c)
            def _():
                leaving[j, piece(k)] = term.astype(jnp.bfloat16)
                earlier = (j - jnp.where(omitted < j, 1, 0)) * pieces + k - WINDOW

                @pl.when(jnp.logical_and(at_end, earlier >= 0))
                def _():
                    sent = jnp.maximum(earlier, 0)
                    slot = lax.div(sent, pieces)
                    sum_copy(slot + jnp.where(omitted <= slot, 1, 0), lax.rem(sent, pieces),
                             0, c).wait_send()

                @pl.when(c == 0)
                def _():
                    send_right(j, k)

                @pl.when(c == chips - 1)
                def _():
                    send_left(j, k, d)

    mine = flip(f, c, bits)
    from_right = flip(f, 0, bits)
    from_left = flip(f, chips - 1, bits)
    slot_right = mine - jnp.where(from_right < mine, 1, 0)
    slot_left = mine - jnp.where(from_left < mine, 1, 0)
    last = jnp.where(c == 0, slot_left, jnp.where(c == chips - 1, slot_right,
                                                  jnp.maximum(slot_left, slot_right)))

    def finish(k):
        @pl.when(c > 0)
        def _():
            sum_copy(mine, k, mine, c).wait_recv()
            total[piece(k)] += arrived[mine, piece(k)].astype(jnp.float32)

        @pl.when(c < chips - 1)
        def _():
            sum_copy(mine, k, groups, c).wait_recv()
            total[piece(k)] += arrived[groups, piece(k)].astype(jnp.float32)

        place = pl.ds(pl.multiple_of(lax.rem(k * rows, table_rows), rows), rows)
        for b in range(own // HD):
            cut = slice(b * HD, (b + 1) * HD)
            value = total[piece(k), cut]
            turned = value * cos_ref[place, cut] + pltpu.roll(value, HD // 2, 1) * sin_ref[place, cut]
            out_ref[piece(k), cut] = turned.astype(out_ref.dtype)

    count = (chips - 1) * pieces

    def at(step, distance):
        index = step - SKEW * distance
        known = jnp.minimum(jnp.maximum(index, 0), count - 1)
        valid = jnp.logical_and(index >= 0, index < count)
        return valid, lax.div(known, pieces), lax.rem(known, pieces)

    @pl.loop(0, count + SKEW * (chips - 1))
    def _(step):
        valid, slot, k_right = at(step, c)
        j_right = slot + jnp.where(from_right <= slot, 1, 0)
        d_right = flip(f, j_right, bits)

        @pl.when(jnp.logical_and(valid, jnp.logical_and(c > 0, d_right > c)))
        def _():
            add_arrived(j_right, k_right)
            send_right(j_right, k_right)

        valid, slot, k_left = at(step, chips - 1 - c)
        j_left = slot + jnp.where(from_left <= slot, 1, 0)
        d_left = flip(f, j_left, bits)

        @pl.when(jnp.logical_and(valid, jnp.logical_and(c < chips - 1, d_left < c)))
        def _():
            add_arrived(j_left, k_left)
            send_left(j_left, k_left, d_left)

        valid, slot, k_own = at(step, chips - 1)

        @pl.when(jnp.logical_and(valid, slot == last))
        def _():
            finish(k_own)

    new_out_ref[...] = collect()
    drain()
    w_copy(0, 1).wait_send()
    for j in range(1, groups):
        for swap in range(2):
            w_copy(j, swap).wait_send()

    @pl.loop(0, pieces)
    def _(k):
        x_copy(k).wait_send()

        @pl.loop(0, groups)
        def _(j):
            index = (j - jnp.where(omitted < j, 1, 0)) * pieces + k
            waiting = jnp.logical_or(jnp.logical_not(at_end), index >= (chips - 1) * pieces - WINDOW)

            @pl.when(jnp.logical_and(flip(f, j, bits) != c, waiting))
            def _():
                sum_copy(j, k, j, c).wait_send()


def recompute_cache(prefix_states, w_keyvalue, cosine, sine_part, new_states, w_query):
    groups, members = lax.axis_size("fsdp"), lax.axis_size("tp")
    chips = members // 2
    assert chips == groups and groups & (groups - 1) == 0
    token_count, depth = prefix_states.shape
    own = w_keyvalue.shape[1] // 2
    pieces = token_count // 256
    fresh_count = new_states.shape[0]
    fresh_width = (w_query.shape[1] + w_keyvalue.shape[1]) * groups // members
    return pl.pallas_call(
        functools.partial(cache_kernel, groups, chips, pieces),
        out_shape=(
            jax.ShapeDtypeStruct((token_count, own), jnp.bfloat16),
            jax.ShapeDtypeStruct((fresh_count, fresh_width), jnp.float32),
        ),
        in_specs=[VMEM] * 6,
        out_specs=(VMEM, VMEM),
        scratch_shapes=[
            pltpu.VMEM((token_count, depth), jnp.bfloat16),
            pltpu.VMEM((groups, 2, depth, own), jnp.bfloat16),
            pltpu.VMEM((groups + 1, token_count, own), jnp.bfloat16),
            pltpu.VMEM((groups, token_count, own), jnp.bfloat16),
            pltpu.VMEM((token_count, own), jnp.float32),
            pltpu.SemaphoreType.DMA((pieces,)),
            pltpu.SemaphoreType.DMA((pieces,)),
            pltpu.SemaphoreType.DMA((groups, 2)),
            pltpu.SemaphoreType.DMA((groups, 2)),
            pltpu.SemaphoreType.DMA((groups, pieces)),
            pltpu.SemaphoreType.DMA((groups + 1, pieces)),
        ] + relay_scratch(groups, members, fresh_count, depth, fresh_width),
        compiler_params=pltpu.CompilerParams(
            collective_id=0, has_side_effects=True, vmem_limit_bytes=60 * 1024 * 1024),
    )(prefix_states, w_keyvalue, cosine, sine_part, new_states, w_query)


def project_kernel(groups, members, x_ref, w_ref, out_ref, x_all, near_out, near_in, far_in, *sems):
    f = lax.axis_index("fsdp")
    t = lax.axis_index("tp")
    barrier = pltpu.get_barrier_semaphore()
    for j in range(1, groups):
        pl.semaphore_signal(barrier, inc=1, device_id=(lax.rem(f + j, groups), t),
                            device_id_type=MESH)
    for i in range(1, members):
        pl.semaphore_signal(barrier, inc=1, device_id=(f, lax.rem(t + i, members)),
                            device_id_type=MESH)
    pl.semaphore_wait(barrier, groups + members - 2)
    gather, multiply, scatter, collect, drain = relay(
        f, t, groups, members, x_ref, x_all, near_out, near_in, far_in, sems)
    gather()
    multiply([w_ref])
    scatter()
    out_ref[...] = collect().astype(out_ref.dtype)
    drain()


def project(x, weight, out_dtype, collective_id):
    groups, members = lax.axis_size("fsdp"), lax.axis_size("tp")
    rows, depth = x.shape
    columns = weight.shape[1] * groups // members
    return pl.pallas_call(
        functools.partial(project_kernel, groups, members),
        out_shape=jax.ShapeDtypeStruct((rows, columns), out_dtype),
        in_specs=[VMEM] * 2,
        out_specs=VMEM,
        scratch_shapes=relay_scratch(groups, members, rows, depth, columns),
        compiler_params=pltpu.CompilerParams(
            collective_id=collective_id, has_side_effects=True, vmem_limit_bytes=32 * 1024 * 1024),
    )(x, weight)


def body(prefix_states, new_states, w_query, w_keyvalue, w_output, lengths):
    my_index = lax.axis_index("tp")
    token_count = prefix_states.shape[0]
    fresh_count = new_states.shape[0]
    seq_lengths = lengths[0]
    score_scale = HD ** (-0.5)
    own_rows = w_keyvalue.shape[1] // 2
    block_count = own_rows // HD
    block_kind = (my_index * block_count + jnp.arange(block_count, dtype=jnp.int32)) % 2
    frequency = theta_base ** (-2.0 * jnp.arange(HD // 2, dtype=jnp.float32) / HD)
    angles = jnp.arange(L, dtype=jnp.int32).astype(jnp.float32)[:, None] * frequency[None, :]
    cosine, sine_part = jnp.cos(angles), jnp.sin(angles)
    is_key = jnp.repeat(block_kind == 0, HD)[None, :]
    cosine = jnp.where(is_key, jnp.tile(cosine, (1, 2 * block_count)), 1.0)
    sine_part = jnp.where(
        is_key, jnp.tile(jnp.concatenate([-sine_part, sine_part], axis=1), (1, block_count)), 0.0
    )
    cache_out, new_sum = recompute_cache(
        prefix_states, w_keyvalue, cosine, sine_part, new_states, w_query
    )
    query_width = new_sum.shape[1] - own_rows
    query_sum, fresh_sum = new_sum[:, :query_width], new_sum[:, query_width:]
    fresh_positions = (
        jnp.repeat(seq_lengths, STEPS) + jnp.tile(jnp.arange(STEPS, dtype=jnp.int32), NSEQ)
    ).astype(jnp.float32)
    fresh_blocks = fresh_sum.reshape(fresh_count, block_count, HD)
    fresh_rotated = rotate(fresh_blocks, fresh_positions)
    fresh_mine = jnp.where((block_kind == 0)[None, :, None], fresh_rotated, fresh_blocks).astype(
        jnp.bfloat16
    )
    if block_count == 1:
        cache_other, fresh_other = partner((cache_out, fresh_mine), "tp", 0)
        holds_keys = my_index % 2 == 0
        key_table = jnp.where(holds_keys, cache_out, cache_other)
        value_table = jnp.where(holds_keys, cache_other, cache_out)
        fresh_keys = jnp.where(holds_keys, fresh_mine[:, 0], fresh_other[:, 0])
        fresh_values = jnp.where(holds_keys, fresh_other[:, 0], fresh_mine[:, 0])
    else:
        key_table = cache_out[:, :HD]
        value_table = cache_out[:, HD:]
        fresh_keys = fresh_mine[:, 0]
        fresh_values = fresh_mine[:, 1]
    local_heads = query_sum.shape[1] // HD
    query_rot = rotate(query_sum.reshape(fresh_count, local_heads, HD), fresh_positions).astype(
        jnp.bfloat16
    )
    query_four = query_rot.reshape(NSEQ, STEPS, local_heads, HD)
    prefix_scores = (
        jnp.einsum(
            "sjhd,sld->sjhl",
            query_four,
            key_table.reshape(NSEQ, L, HD),
            preferred_element_type=jnp.float32,
        )
        * score_scale
    )
    live_keys = jnp.arange(L, dtype=jnp.int32)[None, :] < seq_lengths[:, None]
    prefix_scores = jnp.where(live_keys[:, None, None, :], prefix_scores, masked_score)
    fresh_scores = (
        jnp.einsum(
            "sjhd,sid->sjhi",
            query_four,
            fresh_keys.reshape(NSEQ, STEPS, HD),
            preferred_element_type=jnp.float32,
        )
        * score_scale
    )
    causal = jnp.arange(STEPS)[None, :] <= jnp.arange(STEPS)[:, None]
    fresh_scores = jnp.where(causal[None, :, None, :], fresh_scores, masked_score)
    row_max = jnp.maximum(jnp.max(prefix_scores, axis=-1), jnp.max(fresh_scores, axis=-1))
    prefix_weight = jnp.exp(prefix_scores - row_max[..., None])
    fresh_weight = jnp.exp(fresh_scores - row_max[..., None])
    denominator = jnp.sum(prefix_weight, axis=-1) + jnp.sum(fresh_weight, axis=-1)
    numerator = jnp.einsum(
        "sjhl,sld->sjhd",
        prefix_weight.astype(jnp.bfloat16),
        value_table.reshape(NSEQ, L, HD),
        preferred_element_type=jnp.float32,
    )
    numerator = numerator + jnp.einsum(
        "sjhi,sid->sjhd",
        fresh_weight.astype(jnp.bfloat16),
        fresh_values.reshape(NSEQ, STEPS, HD),
        preferred_element_type=jnp.float32,
    )
    attended = (
        (numerator / denominator[..., None])
        .reshape(fresh_count, local_heads * HD)
        .astype(jnp.bfloat16)
    )
    return (cache_out, project(attended, w_output, jnp.bfloat16, 1))


def solution(mesh):
    in_specs = (
        P("fsdp", "tp"),
        P("fsdp", "tp"),
        P("tp", "fsdp"),
        P("tp", "fsdp"),
        P("tp", "fsdp"),
        P("fsdp", None),
    )
    out_specs = (P("fsdp", "tp"), P("fsdp", "tp"))
    return jax.shard_map(body, mesh=mesh, in_specs=in_specs, out_specs=out_specs, check_vma=False)
```
